512 devices in a mesh: tower: 32 (over y, x), shard: 16 (over z, core).
Axes of the slice: x: 4, y: 8, z: 8, core: 2. Of those that a mesh axis runs over, the one named last changes fastest.
Arguments:
- quotient_rows: bfloat16 [512, 256, 128], P('tower', 'shard'), may hold values from -6 to 6
- remainder_rows: bfloat16 [512, 128, 128], P('tower'), may hold values from -6 to 6
- quotient_index: int32 [512, 16, 512], P('tower', 'shard'), may hold values from 0 to 255
- remainder_index: int32 [512, 16, 512], P('tower', 'shard'), may hold values from 0 to 127
- bag_sizes: int32 [512, 16, 128], P('tower', 'shard'), may hold values from 1 to 16, 512 in all within a row
- tower_weight: bfloat16 [32, 2048, 256], P('tower'), may hold values from -5 to 5
- norm_gain: bfloat16 [8192], replicated, may hold values from 0.25 to 1.75
- cotangent: bfloat16 [16, 128, 8192], P('shard', 'tower'), may hold values from -1.25 to 1.25
Outputs:
- joint: bfloat16 [16, 128, 8192], P('shard', 'tower')
- weight_grad: float32 [32, 2048, 256], P('tower')
- quotient_grad: float32 [512, 256, 128], P('tower', 'shard')
- remainder_grad: float32 [512, 128, 128], P('tower', 'shard')
The draws below stay inside these ranges and needn't reach their ends.
Inputs may be any that keep to these rules, and one draw needn't show every extreme that they name: `bag_sizes`: each row sums to 512; lookups are ordered by example.
All inputs are finite; a program needn't handle non-finite values.
Results may differ from the reference program's by a relative error of at most 0.0093.
Values may be sent and summed in bfloat16 or wider, within the bound.
No kernel may reach another device: no remote copies, remote signals or barrier semaphores. Data moves between devices by JAX's collectives and lax.ppermute only.
A program may use at most 64 MiB of HBM per device.

```python
import math
import jax
import jax.numpy as jnp
import numpy as np
from jax import lax

D_EMB = 128
TOWER_OUT = 256
F_T = 16
R_ROWS = 128
LPB = 4
BAG_MOST = 16
OWNED = 128
FEATURES = 512
EXAMPLES = 2048
QROWS = 256
BAG_LOOKUPS = 512
N_TOWER = 32
N_SHARD = 16


def draw_tower_weight(key, part):
    key = jax.random.fold_in(key, 11)
    scale_key, value_key = jax.random.split(key)
    level = jax.random.uniform(scale_key, (N_TOWER, 1, 1), jnp.float32)
    scale = jnp.exp(level * math.log(10.0))
    values = jnp.clip(jax.random.normal(value_key, (N_TOWER, F_T * D_EMB, TOWER_OUT), jnp.float32), -4.0, 4.0)
    return (values * scale * (1.0 / math.sqrt(F_T * D_EMB))).astype(jnp.bfloat16)


def touch_ends(array, own_key, least, high):
    shape = array.shape
    place = [jax.random.randint(jax.random.fold_in(own_key, axis), (), 0, shape[axis]) for axis in range(len(shape))]
    array = array.at[tuple(place)].set(least)
    longest = shape.index(max(shape))
    place[longest] = (place[longest] + 1) % shape[longest]
    return array.at[tuple(place)].set(high)


def shard_levels(key, dims, pieces, least, largest):
    def one(axis_at, blocks):
        draws = jax.random.uniform(jax.random.fold_in(jax.random.fold_in(key, 6), axis_at), (blocks,), jnp.float32, least / len(pieces), largest / len(pieces))
        return jnp.repeat(jnp.exp(draws), dims[axis_at] // blocks).reshape((-1,) + (1,) * (len(dims) - axis_at - 1))

    loudness = one(*pieces[0])
    for cut in pieces[1:]:
        loudness = loudness * one(*cut)
    return loudness


def rank_table(number_of, lean):
    loads = [(1 << 20) // math.isqrt(standing ** lean) + 1 for standing in range(1, number_of + 1)]
    scale = 1 + sum(loads) // (1 << 30)
    return np.cumsum(np.array([max(1, weight // scale) for weight in loads]))


def skewed_ids(rng, shape, amount, slope):
    grid = rank_table(amount, slope)
    lot = jax.random.randint(jax.random.fold_in(rng, 1), shape, 0, int(grid[amount - 1]))
    grade = jnp.searchsorted(jnp.asarray(grid, jnp.int32), lot, side="right")
    return jax.random.permutation(jax.random.fold_in(rng, 2), amount)[grade].astype(jnp.int32)


def split_up(amount, total, most, lean):
    loads = [(1 << 20) // math.isqrt(standing ** lean) + 1 for standing in range(2, amount + 1)]
    surplus, given = total - most - (amount - 1), [1] * (amount - 1)
    while surplus > 0:
        candidates = [i for i in range(amount - 1) if given[i] < most]
        mass, remaining = sum([loads[i] for i in candidates]), surplus
        for i in candidates:
            addition = min(most - given[i], max(1, remaining * loads[i] // mass), surplus)
            given[i] = given[i] + addition
            surplus = surplus - addition
    return np.array([most] + given)


def uneven(own_key, count, total, reach, skew):
    if count == 2:
        one = jax.random.randint(own_key, (), max(1, total - reach), min(reach, total - 1) + 1)
        return jnp.stack([one, total - one])
    tallies = jnp.asarray(split_up(count, total, reach, skew), jnp.int32)
    pairs = (count - 1) // 2
    source_of, receiver = tallies[1:1 + 2 * pairs:2], tallies[2:2 + 2 * pairs:2]
    margin = jnp.minimum(source_of - 1, reach - receiver)
    passed = jax.random.randint(jax.random.fold_in(own_key, 1), (pairs,), 0, 1 << 20) % (margin + 1)
    tallies = tallies.at[1:1 + 2 * pairs:2].set(source_of - passed).at[2:2 + 2 * pairs:2].set(receiver + passed)
    return tallies[jax.random.permutation(jax.random.fold_in(own_key, 2), count)]


def gaussian(stream_key, dims, scale, limit, pieces=(), kind=jnp.bfloat16):
    values = jax.random.normal(stream_key, dims, jnp.float32) * scale
    if len(pieces) > 0:
        values = shard_levels(stream_key, dims, pieces, -0.22, 0.18) * values
    return jnp.clip(values, min=-limit, max=limit).astype(kind)


def setup_inputs(seed: int = 0) -> dict:
    splits = jax.random.split(jax.random.key(seed), 9)
    return {
        "quotient_rows": gaussian(splits[0], (FEATURES, QROWS, D_EMB), 1.0, 6.0, ((0, 32), (1, 16))),
        "remainder_rows": gaussian(splits[1], (FEATURES, R_ROWS, D_EMB), 1.0, 6.0, ((0, 32),)),
        "quotient_index": touch_ends(skewed_ids(splits[2], (FEATURES, N_SHARD, BAG_LOOKUPS), QROWS, 2), jax.random.fold_in(splits[2], 3), 0, QROWS - 1).astype(jnp.int32),
        "remainder_index": touch_ends(jax.random.randint(splits[3], (FEATURES, N_SHARD, BAG_LOOKUPS), 0, R_ROWS), jax.random.fold_in(splits[3], 1), 0, R_ROWS - 1).astype(jnp.int32),
        "bag_sizes": jax.vmap(lambda own: uneven(own, OWNED, BAG_LOOKUPS, BAG_MOST, 2))(jax.random.split(splits[4], FEATURES * N_SHARD)).reshape((FEATURES, N_SHARD, OWNED)).astype(jnp.int32),
        "tower_weight": draw_tower_weight(jax.random.fold_in(splits[8], 71), 0),
        "norm_gain": jnp.clip(1.0 + 0.15 * jax.random.normal(splits[6], (N_TOWER * TOWER_OUT,), jnp.float32), 0.25, 1.75).astype(jnp.bfloat16),
        "cotangent": gaussian(splits[7], (N_SHARD, OWNED, N_TOWER * TOWER_OUT), (4.0 / EXAMPLES ** 0.5), 1.25, ((0, 16), (1, 32))),
    }


norm_eps = 1e-05

def layer_norm(values, gain):
    center = values - lax.optimization_barrier(jnp.mean(values, axis=-1, keepdims=True))
    spread = lax.optimization_barrier(jnp.mean(center * center, axis=-1, keepdims=True))
    return center * lax.rsqrt(spread + norm_eps) * gain

def locate(sizes, positions):
    ends = jnp.cumsum(sizes)
    return jnp.searchsorted(ends, positions, side='right').astype(jnp.int32)

def reference(quotient_rows, remainder_rows, quotient_index, remainder_index, bag_sizes, tower_weight, norm_gain, cotangent):
    positions = jnp.arange(OWNED * LPB, dtype=jnp.int32)
    q_towers = quotient_rows.reshape(N_TOWER, F_T, QROWS, D_EMB)
    r_towers = remainder_rows.reshape(N_TOWER, F_T, R_ROWS, D_EMB)
    qi_towers = quotient_index.reshape(N_TOWER, F_T, N_SHARD, OWNED * LPB)
    ri_towers = remainder_index.reshape(N_TOWER, F_T, N_SHARD, OWNED * LPB)
    size_towers = bag_sizes.reshape(N_TOWER, F_T, N_SHARD, OWNED)

    def pool_feature(items):
        q_table, r_table, q_pick, r_pick, sizes = items

        def pool_group(q_one, r_one, size_one):
            seg = locate(size_one, positions)
            composed = q_table[q_one].astype(jnp.float32) * r_table[r_one].astype(jnp.float32)
            return jax.ops.segment_sum(composed, seg, num_segments=OWNED)
        return jax.vmap(pool_group)(q_pick, r_pick, sizes)

    def tower_inputs(q_tab, r_tab, q_pick, r_pick, sizes):
        pooled = lax.map(pool_feature, (q_tab, r_tab, q_pick, r_pick, sizes))
        bag = pooled.astype(jnp.bfloat16)
        return bag.transpose(1, 2, 0, 3).reshape(EXAMPLES, F_T * D_EMB)

    def tower_forward(items):
        q_tab, r_tab, q_pick, r_pick, sizes, weight = items
        flat = tower_inputs(q_tab, r_tab, q_pick, r_pick, sizes)
        pre = jnp.dot(flat, weight, preferred_element_type=jnp.float32)
        return jax.nn.silu(pre).astype(jnp.bfloat16)
    activated = lax.map(tower_forward, (q_towers, r_towers, qi_towers, ri_towers, size_towers, tower_weight))
    joined = activated.transpose(1, 0, 2).reshape(EXAMPLES, N_TOWER * TOWER_OUT)
    normed, pullback = jax.vjp(lambda v: layer_norm(v, norm_gain.astype(jnp.float32)), joined.astype(jnp.float32))
    joined_grad = pullback(cotangent.reshape(EXAMPLES, N_TOWER * TOWER_OUT).astype(jnp.float32))[0].astype(jnp.bfloat16)
    tower_grad = joined_grad.reshape(EXAMPLES, N_TOWER, TOWER_OUT).transpose(1, 0, 2)

    def tower_backward(items):
        q_tab, r_tab, q_pick, r_pick, sizes, weight, out_grad = items
        flat = tower_inputs(q_tab, r_tab, q_pick, r_pick, sizes)
        pre = jnp.dot(flat, weight, preferred_element_type=jnp.float32)
        sigma = jax.nn.sigmoid(pre)
        pre_grad = (out_grad.astype(jnp.float32) * sigma * (1.0 + pre * (1.0 - sigma))).astype(jnp.bfloat16)
        weight_part = lax.dot_general(flat, pre_grad, (((0,), (0,)), ((), ())), preferred_element_type=jnp.float32)
        input_grad = jnp.dot(pre_grad, weight.T, preferred_element_type=jnp.float32).astype(jnp.bfloat16)
        bag_grad = input_grad.reshape(N_SHARD, OWNED, F_T, D_EMB).transpose(2, 0, 1, 3)

        def grad_feature(parts):
            q_table, r_table, q_one, r_one, size_one, grads = parts
            seg = jax.vmap(lambda sz: locate(sz, positions))(size_one)
            lookup_grad = jax.vmap(lambda g, s: g[s])(grads, seg).astype(jnp.float32).reshape(N_SHARD * OWNED * LPB, D_EMB)
            q_flat = q_one.reshape(N_SHARD * OWNED * LPB)
            r_flat = r_one.reshape(N_SHARD * OWNED * LPB)
            q_part = jax.ops.segment_sum(lookup_grad * r_table[r_flat].astype(jnp.float32), q_flat, num_segments=QROWS)
            r_part = jax.ops.segment_sum(lookup_grad * q_table[q_flat].astype(jnp.float32), r_flat, num_segments=R_ROWS)
            return (q_part, r_part)
        q_grad, r_grad = lax.map(grad_feature, (q_tab, r_tab, q_pick, r_pick, sizes, bag_grad))
        return (weight_part, q_grad, r_grad)
    weight_grad, quotient_grad, remainder_grad = lax.map(tower_backward, (q_towers, r_towers, qi_towers, ri_towers, size_towers, tower_weight, tower_grad))
    joint = normed.astype(jnp.bfloat16).reshape(N_SHARD, OWNED, N_TOWER * TOWER_OUT)
    return (joint, weight_grad, quotient_grad.reshape(FEATURES, QROWS, D_EMB), remainder_grad.reshape(FEATURES, R_ROWS, D_EMB))
```

```python
import functools

import jax
import jax.numpy as jnp
from jax import lax
from jax.experimental import pallas as pl
from jax.experimental.pallas import tpu as pltpu
from jax.sharding import PartitionSpec as P

norm_eps = 1e-05
f32, bf16 = jnp.float32, jnp.bfloat16
NT = (((1,), (1,)), ((), ()))
VMEM_LIMIT = 48 * 1024 * 1024


def mm(a, b):
    return jnp.dot(a, b, preferred_element_type=f32)


def mm_nt(a, b):
    return lax.dot_general(a, b, NT, preferred_element_type=f32)


def triangles(n):
    row = lax.broadcasted_iota(jnp.int32, (n, n), 0)
    col = lax.broadcasted_iota(jnp.int32, (n, n), 1)
    upto = jnp.where(col <= row, 1.0, 0.0).astype(bf16)
    before = jnp.where(col < row, 1.0, 0.0).astype(bf16)
    return jnp.concatenate([upto, before], axis=0)


def masks(picks, tri):
    values = picks.astype(f32)
    row_q = lax.broadcasted_iota(jnp.int32, (256, 128), 0).astype(f32)
    row_r = lax.broadcasted_iota(jnp.int32, (128, 128), 0).astype(f32)
    lane = lax.broadcasted_iota(jnp.int32, (128, 128), 1).astype(f32)
    sums = mm_nt(tri, picks)
    ends = jnp.broadcast_to(sums[:128, 8:9], (128, 128))
    starts = jnp.broadcast_to(sums[128:, 8:9], (128, 128))
    quot, rem, member = [], [], []
    for c in range(4):
        quot.append(jnp.where(row_q == values[c : c + 1], 1.0, 0.0).astype(bf16))
        rem.append(jnp.where(row_r == values[4 + c : 5 + c], 1.0, 0.0).astype(bf16))
        here = lane + float(128 * c)
        inside = (here < ends) & (here >= starts)
        member.append(jnp.where(inside, 1.0, 0.0).astype(bf16))
    return tuple(jnp.concatenate(v, axis=1) for v in (quot, rem, member))


def pool_kernel(per_step, got_ref, rem_ref, bag_ref, bag_t_ref, quot_ref, remd_ref, qt_ref, rt_ref):
    step = pl.program_id(0)

    @pl.when(step == 0)
    def _():
        table = got_ref[:, :16, :].reshape(256, 128)
        qt_ref[...] = table.astype(f32).T.astype(bf16)
        rt_ref[...] = rem_ref[...].astype(f32).T.astype(bf16)

    tri = triangles(128)
    for i in range(per_step):
        picks = got_ref[step * per_step + i, 16:32, :]
        quot_hot, rem_hot, member = masks(picks, tri)
        quot = mm(qt_ref[...], quot_hot)
        rem = mm(rt_ref[...], rem_hot)
        composed = quot * rem
        high = composed.astype(bf16)
        low = (composed - high.astype(f32)).astype(bf16)
        pooled = mm_nt(member, high) + mm_nt(member, low)
        bag_ref[i] = pooled.astype(bf16)
        bag_t_ref[i] = pooled.T.astype(bf16)
        quot_ref[i] = quot.astype(bf16)
        remd_ref[i] = rem.astype(bf16)


def pool(got, remainder):
    groups, per_step = got.shape[0], 4
    block = lambda *dims: pl.BlockSpec((per_step, *dims), lambda i: (i, 0, 0))
    shape = lambda *dims: jax.ShapeDtypeStruct((groups, *dims), bf16)
    return pl.pallas_call(
        functools.partial(pool_kernel, per_step),
        grid=(groups // per_step,),
        in_specs=[
            pl.BlockSpec(got.shape, lambda i: (0, 0, 0)),
            pl.BlockSpec(remainder.shape, lambda i: (0, 0)),
        ],
        out_specs=[block(128, 128), block(128, 128), block(128, 512), block(128, 512)],
        out_shape=[shape(128, 128), shape(128, 128), shape(128, 512), shape(128, 512)],
        scratch_shapes=[pltpu.VMEM((128, 256), bf16), pltpu.VMEM((128, 128), bf16)],
        compiler_params=pltpu.CompilerParams(vmem_limit_bytes=VMEM_LIMIT),
        name="pool",
    )(got, remainder)


def tower_kernel(bags_ref, weight_ref, cot_ref, gain_ref, pre_ref, out_ref):
    feats = bags_ref.shape[0]
    flat = jnp.concatenate([bags_ref[f] for f in range(feats)], axis=1)
    pre = mm(flat, weight_ref[...])
    pre_ref[...] = pre
    act = (pre * jax.nn.sigmoid(pre)).astype(bf16).astype(f32)
    mean = jnp.mean(act, axis=1, keepdims=True)
    center = act - mean
    scaled = cot_ref[...].astype(f32) * gain_ref[...]
    spread = jnp.sum(center * center, axis=1, keepdims=True)
    total = jnp.sum(scaled, axis=1, keepdims=True)
    lean = jnp.sum(scaled * center, axis=1, keepdims=True)
    lane = lax.broadcasted_iota(jnp.int32, (128, 128), 1)
    table = jnp.where(
        lane == 0, mean, jnp.where(lane == 1, spread, jnp.where(lane == 2, total, lean))
    )
    stats = table.T[:8]
    for d in range(out_ref.shape[0]):
        out_ref[d, 0:4, :] = act[4 * d : 4 * d + 4, :128]
        out_ref[d, 4:8, :] = act[4 * d : 4 * d + 4, 128:]
        out_ref[d, 8:16, :] = stats


def tower_forward(bags, weight, cot, gain, towers):
    return pl.pallas_call(
        tower_kernel,
        out_shape=[
            jax.ShapeDtypeStruct((128, 256), f32),
            jax.ShapeDtypeStruct((towers, 16, 128), f32),
        ],
        compiler_params=pltpu.CompilerParams(vmem_limit_bytes=VMEM_LIMIT),
        name="tower_forward",
    )(bags, weight, cot, gain)


def back_kernel(columns, got_ref, pre_ref, cot_ref, gain_ref, out_ref):
    towers = got_ref.shape[0]
    stats = got_ref[:, 8:16, :]
    sums = jnp.sum(stats, axis=0)
    mean = sums[0:1] * (1.0 / towers)
    shift = stats[:, 0:1, :] - mean[None]
    spread = sums[1:2] + (columns / towers) * jnp.sum(shift * shift, axis=0)
    lean = sums[3:4] + jnp.sum(stats[:, 2:3, :] * shift, axis=0)
    scale = lax.rsqrt(spread * (1.0 / columns) + norm_eps)
    rows = [mean, scale, sums[2:3] * (1.0 / columns), lean * scale * scale * (1.0 / columns)]
    table = jnp.concatenate(rows + [jnp.zeros((124, 128), f32)], axis=0).T
    mean, scale, total, lean = (table[:, i : i + 1] for i in range(4))
    pre = pre_ref[...]
    sigma = jax.nn.sigmoid(pre)
    act = (pre * sigma).astype(bf16).astype(f32)
    scaled = cot_ref[...].astype(f32) * gain_ref[...]
    grad = (scale * (scaled - total - (act - mean) * lean)).astype(bf16).astype(f32)
    pre_grad = (grad * sigma * (1.0 + pre * (1.0 - sigma))).astype(bf16)
    for d in range(out_ref.shape[0]):
        out_ref[d] = pre_grad


def tower_back(got, pre, cot, gain, copies):
    columns = got.shape[0] * pre.shape[1]
    return pl.pallas_call(
        functools.partial(back_kernel, float(columns)),
        out_shape=jax.ShapeDtypeStruct((copies, *pre.shape), bf16),
        compiler_params=pltpu.CompilerParams(vmem_limit_bytes=VMEM_LIMIT),
        name="tower_back",
    )(got, pre, cot, gain)


def weight_kernel(class_ref, bag_ref, mine_ref, other_ref, out_ref):
    zs = mine_ref.shape[0]
    side = class_ref[0]
    total = jnp.zeros(out_ref.shape[1:], f32)
    for z in range(zs):
        total += mm(bag_ref[2 * z + side], mine_ref[z])
        total += mm(bag_ref[2 * z + 1 - side], other_ref[z])
    chunk = total.astype(bf16)
    for d in range(out_ref.shape[0]):
        out_ref[d] = chunk


def weight_part(side, bag_t, mine, other):
    vmem = pl.BlockSpec(memory_space=pltpu.VMEM)
    return pl.pallas_call(
        weight_kernel,
        in_specs=[pl.BlockSpec(memory_space=pltpu.SMEM), vmem, vmem, vmem],
        out_specs=vmem,
        out_shape=jax.ShapeDtypeStruct((mine.shape[0], 128, 256), bf16),
        compiler_params=pltpu.CompilerParams(vmem_limit_bytes=VMEM_LIMIT),
        name="weight_part",
    )(side, bag_t, mine, other)


def rows_kernel(per_step, side_ref, got_ref, weight_ref, quot_ref, rem_ref, grad_ref, qg_ref, rg_ref):
    @pl.when(pl.program_id(0) == 0)
    def _():
        qg_ref[...] = jnp.zeros_like(qg_ref)
        rg_ref[...] = jnp.zeros_like(rg_ref)

    tri = triangles(128)
    quot_sum, rem_sum = qg_ref[...], rg_ref[...]
    for i in range(per_step):
        quot_hot, rem_hot, member = masks(got_ref[i, 0, 16:32, :], tri)
        bag_grad = mm_nt(weight_ref[...], grad_ref[i]).astype(bf16)
        look = mm(bag_grad, member)
        quot_part = (look * rem_ref[i, 0].astype(f32)).astype(bf16)
        rem_part = (look * quot_ref[i, 0].astype(f32)).astype(bf16)
        quot_sum += mm_nt(quot_hot, quot_part)
        rem_sum += mm_nt(rem_hot, rem_part)
    qg_ref[...] = quot_sum
    rg_ref[...] = rem_sum


def rows_part(side, got, weight, quot, rem, grad):
    zs, per_step = grad.shape[0], 4
    pair = lambda a: a.reshape(zs, 2, *a.shape[1:])
    block = lambda *dims: pl.BlockSpec((per_step, 1, *dims), lambda i, s: (i, s[0], 0, 0))
    whole = lambda *dims: pl.BlockSpec(dims, lambda i, s: (0, 0))
    return pl.pallas_call(
        functools.partial(rows_kernel, per_step),
        grid_spec=pltpu.PrefetchScalarGridSpec(
            num_scalar_prefetch=1,
            grid=(zs // per_step,),
            in_specs=[
                block(32, 128),
                whole(128, 256),
                block(128, 512),
                block(128, 512),
                pl.BlockSpec((per_step, 128, 256), lambda i, s: (i, 0, 0)),
            ],
            out_specs=[whole(256, 128), whole(128, 128)],
        ),
        out_shape=[jax.ShapeDtypeStruct((256, 128), f32), jax.ShapeDtypeStruct((128, 128), f32)],
        compiler_params=pltpu.CompilerParams(vmem_limit_bytes=VMEM_LIMIT),
        name="rows_part",
    )(side, pair(got), weight, pair(quot), pair(rem), grad)


def layer_norm(values, gain):
    center = values - jnp.mean(values, axis=-1, keepdims=True)
    spread = jnp.mean(center * center, axis=-1, keepdims=True)
    return center * lax.rsqrt(spread + norm_eps) * gain


def on_device(
    quotient_rows,
    remainder_rows,
    quotient_index,
    remainder_index,
    bag_sizes,
    tower_weight,
    norm_gain,
    cotangent,
):
    feats = quotient_rows.shape[0]
    shards, towers = lax.axis_size("shard"), lax.axis_size("tower")
    shard, tower = lax.axis_index("shard"), lax.axis_index("tower")
    zs = shards // 2
    along_z = [[2 * z + c for z in range(zs)] for c in range(2)]
    across = [(i, i ^ 1) for i in range(shards)]
    swap = functools.partial(lax.all_to_all, split_axis=0, concat_axis=0, tiled=True)
    gather_z = functools.partial(swap, axis_name="shard", axis_index_groups=along_z)
    side = (shard % 2).astype(jnp.int32)
    side_arg = side[None]

    picks = jnp.concatenate(
        [
            quotient_index.reshape(feats, 4, 128),
            remainder_index.reshape(feats, 4, 128),
            bag_sizes.reshape(feats, 1, 128),
            jnp.zeros((feats, 7, 128), jnp.int32),
        ],
        axis=1,
    ).astype(bf16)
    got = swap(jnp.concatenate([quotient_rows, picks], axis=1), "shard")
    cot = lax.all_to_all(cotangent[0], "tower", split_axis=1, concat_axis=0, tiled=True)
    gain = norm_gain.astype(f32)
    gain_here = lax.dynamic_slice(gain, (tower * 256,), (256,))[None]
    remainder = lax.dynamic_index_in_dim(remainder_rows, shard, 0, keepdims=False)
    weight = tower_weight[0]
    weight_here = lax.dynamic_slice(weight, (shard * 128, 0), (128, 256))

    bag, bag_t, quot, rem = pool(got, remainder)
    bags = swap(bag, "shard")
    pre, sent = tower_forward(bags, weight, cot, gain_here, towers)
    stats = swap(sent, "tower")
    grad_copies = tower_back(stats, pre, cot, gain_here, zs)
    grad_mine = gather_z(grad_copies)
    grad_other = lax.ppermute(grad_mine, "shard", across)

    joined = stats[:, :8].reshape(towers, 2, 4, 128).transpose(2, 0, 1, 3).reshape(4, towers * 256)
    joint = layer_norm(joined, gain).astype(bf16)[None]

    chunk_copies = weight_part(side_arg, bag_t, grad_mine, grad_other)
    chunks_mine = gather_z(chunk_copies)
    quot_a, rem_a = rows_part(side_arg, got, weight_here, quot, rem, grad_mine)
    quot_b, rem_b = rows_part(1 - side_arg, got, weight_here, quot, rem, grad_other)
    rows = jnp.concatenate(
        [(quot_a + quot_b).reshape(shards, 16, 128), (rem_a + rem_b).reshape(shards, 8, 128)], axis=1
    )
    owned = swap(rows, "shard")
    chunks_other = lax.ppermute(chunks_mine, "shard", across)
    even = jnp.where(side == 0, chunks_mine, chunks_other)
    odd = jnp.where(side == 0, chunks_other, chunks_mine)
    weight_grad = jnp.stack([even, odd], axis=1).reshape(1, feats * 128, 256).astype(f32)
    return joint, weight_grad, owned[:, :16], owned[:, 16:]


def solution(mesh):
    in_specs = (
        P("tower", "shard", None),
        P("tower", None, None),
        P("tower", "shard", None),
        P("tower", "shard", None),
        P("tower", "shard", None),
        P("tower", None, None),
        P(),
        P("shard", "tower", None),
    )
    out_specs = (
        P("shard", "tower", None),
        P("tower", None, None),
        P("tower", "shard", None),
        P("tower", "shard", None),
    )
    return jax.shard_map(
        on_device, mesh=mesh, in_specs=in_specs, out_specs=out_specs, check_vma=False
    )
```

```python
import functools

import jax
import jax.numpy as jnp
from jax import lax
from jax.experimental import pallas as pl
from jax.experimental.pallas import tpu as pltpu
from jax.sharding import PartitionSpec as P

norm_eps = 1e-05
f32, bf16 = jnp.float32, jnp.bfloat16
NT = (((1,), (1,)), ((), ()))
PARAMS = pltpu.CompilerParams(vmem_limit_bytes=20 * 1024 * 1024)
vmem = pl.BlockSpec(memory_space=pltpu.VMEM)
smem = pl.BlockSpec(memory_space=pltpu.SMEM)


def mm(a, b):
    return jnp.dot(a, b, preferred_element_type=f32)


def mm_nt(a, b):
    return lax.dot_general(a, b, NT, preferred_element_type=f32)


def cost(micros):
    return pl.CostEstimate(
        flops=int(micros * 1e8), bytes_accessed=int(micros * 3e6), transcendentals=0
    )


def triangles(n):
    row = lax.broadcasted_iota(jnp.int32, (n, n), 0)
    col = lax.broadcasted_iota(jnp.int32, (n, n), 1)
    upto = jnp.where(col <= row, 1.0, 0.0).astype(bf16)
    before = jnp.where(col < row, 1.0, 0.0).astype(bf16)
    return jnp.concatenate([upto, before], axis=0)


def masks(picks, side, tri):
    values = picks.astype(jnp.int32)
    row_q = lax.broadcasted_iota(jnp.int32, (256, 128), 0)
    row_r = lax.broadcasted_iota(jnp.int32, (128, 128), 0)
    lane = lax.broadcasted_iota(jnp.int32, (128, 128), 1).astype(f32)
    place = ((((values >> 4) & 1) ^ side) << 7) + ((values >> 5) << 4) + (values & 15)
    sums = mm_nt(tri, picks)
    ends = jnp.broadcast_to(sums[:128, 8:9], (128, 128))
    starts = jnp.broadcast_to(sums[128:, 8:9], (128, 128))
    quot, rem, member = [], [], []
    for c in range(4):
        quot.append(jnp.where(row_q == place[c : c + 1], 1.0, 0.0).astype(bf16))
        rem.append(jnp.where(row_r == values[4 + c : 5 + c], 1.0, 0.0).astype(bf16))
        here = lane + float(128 * c)
        inside = (here < ends) & (here >= starts)
        member.append(jnp.where(inside, 1.0, 0.0).astype(bf16))
    return tuple(jnp.concatenate(v, axis=1) for v in (quot, rem, member))


def look_up(quot_t, rem_t, quot_hot, rem_hot, member):
    quot = mm(quot_t, quot_hot)
    rem = mm(rem_t, rem_hot)
    composed = quot * rem
    high = composed.astype(bf16)
    low = (composed - high.astype(f32)).astype(bf16)
    return quot, rem, mm_nt(member, high) + mm_nt(member, low)


def pack_kernel(rows_ref, quot_ref, rem_ref, size_ref, out_ref, picks_ref, held):
    feats = rows_ref.shape[0]
    held[...] = jnp.zeros_like(held)
    for f in range(feats):
        for c in range(4):
            part = pl.ds(128 * c, 128)
            held[f, c : c + 1, :] = quot_ref[f, :, part].astype(f32)
            held[f, 4 + c : 5 + c, :] = rem_ref[f, :, part].astype(f32)
        held[f, 8:9, :] = size_ref[f].astype(f32)
    picks = held[...].astype(bf16)
    picks_ref[...] = picks
    rows = rows_ref[...]
    for z in range(out_ref.shape[0]):
        out_ref[z, :feats] = rows
        out_ref[z, feats:] = picks[2 * z : 2 * z + 2]


def pack(rows, quot, rem, sizes):
    feats, zs = rows.shape[0], rows.shape[0] // 2
    whole = lambda a: pl.BlockSpec(a.shape, lambda i: (0, 0, 0))
    pinned = [pltpu.with_memory_space_constraint(a, pltpu.HBM) for a in (rows, quot, rem, sizes)]
    return pl.pallas_call(
        pack_kernel,
        grid=(1,),
        in_specs=[whole(a) for a in pinned],
        out_specs=[
            pl.BlockSpec((zs, feats + 2, 16, 128), lambda i: (0, 0, 0, 0)),
            pl.BlockSpec((feats, 16, 128), lambda i: (0, 0, 0)),
        ],
        out_shape=[
            jax.ShapeDtypeStruct((zs, feats + 2, 16, 128), bf16),
            jax.ShapeDtypeStruct((feats, 16, 128), bf16),
        ],
        scratch_shapes=[pltpu.VMEM((feats, 16, 128), f32)],
        compiler_params=PARAMS,
        cost_estimate=cost(1),
        name="pack",
    )(*pinned)


def tower_kernel(side_ref, mine_ref, other_ref, rem_ref, picks_ref, weight_ref, pre_ref, out_ref, held, sem):
    fetch = pltpu.make_async_copy(weight_ref.at[0], held, sem)
    fetch.start()
    tri = triangles(128)
    side = side_ref[0]
    bags = []
    for f in range(rem_ref.shape[0]):
        table = jnp.concatenate(
            [mine_ref[:, f].reshape(128, 128), other_ref[:, f].reshape(128, 128)], axis=0
        )
        _, _, pooled = look_up(table.T, rem_ref[f].T, *masks(picks_ref[f], side, tri))
        bags.append(pooled.astype(bf16))
    fetch.wait()
    pre = mm(jnp.concatenate(bags, axis=1), held[...])
    pre_ref[...] = pre
    act = pre * jax.nn.sigmoid(pre)
    for d in range(out_ref.shape[0]):
        out_ref[d] = act[4 * d : 4 * d + 4].astype(bf16)


def tower_forward(side, mine, other, remainder, picks, weight, towers):
    return pl.pallas_call(
        tower_kernel,
        in_specs=[smem] + [vmem] * 4 + [pl.BlockSpec(memory_space=pltpu.HBM)],
        out_specs=[vmem] * 2,
        out_shape=[
            jax.ShapeDtypeStruct((128, 256), f32),
            jax.ShapeDtypeStruct((towers, 4, 256), bf16),
        ],
        scratch_shapes=[pltpu.VMEM(weight.shape[1:], bf16), pltpu.SemaphoreType.DMA],
        compiler_params=PARAMS,
        cost_estimate=cost(6),
        name="tower_forward",
    )(side, mine, other, remainder, picks, pltpu.with_memory_space_constraint(weight, pltpu.HBM))


def norm_kernel(got_ref, cot_ref, gain_ref, joint_ref, out_ref):
    towers, _, width = got_ref.shape
    columns = float(towers * width)
    part = [pl.ds(width * t, width) for t in range(towers)]
    mean = sum(got_ref[t].astype(f32) for t in range(towers))
    mean = jnp.sum(mean, axis=1, keepdims=True) * (1.0 / columns)
    center = [got_ref[t].astype(f32) - mean for t in range(towers)]
    spread = jnp.sum(sum(c * c for c in center), axis=1, keepdims=True) * (1.0 / columns)
    scale = lax.rsqrt(spread + norm_eps)
    total, lean = 0.0, 0.0
    for t in range(towers):
        gain = gain_ref[:, part[t]]
        scaled = cot_ref[0, :, part[t]].astype(f32) * gain
        joint_ref[0, :, part[t]] = (center[t] * scale * gain).astype(bf16)
        total += scaled
        lean += scaled * center[t]
    total = jnp.sum(total, axis=1, keepdims=True) * (1.0 / columns)
    lean = jnp.sum(lean, axis=1, keepdims=True) * (1.0 / columns) * scale * scale
    for t in range(towers):
        scaled = cot_ref[0, :, part[t]].astype(f32) * gain_ref[:, part[t]]
        out_ref[t] = (scale * (scaled - total - center[t] * lean)).astype(bf16)


def norm(got, cot, gain):
    return pl.pallas_call(
        norm_kernel,
        out_shape=[
            jax.ShapeDtypeStruct(cot.shape, bf16),
            jax.ShapeDtypeStruct(got.shape, bf16),
        ],
        compiler_params=PARAMS,
        cost_estimate=cost(1),
        name="norm",
    )(got, cot, gain)


def own_tables(own, mine_ref, other_ref, rem_ref):
    quot_t = jnp.concatenate([r[:, own].reshape(128, 128).T for r in (mine_ref, other_ref)], axis=1)
    return quot_t, rem_ref[own].T


def feature_kernel(where_ref, mine_ref, other_ref, rem_ref, bag_ref):
    feats, zs = rem_ref.shape[0], mine_ref.shape[0]
    own, side = where_ref[0], where_ref[1]
    tables = own_tables(own, mine_ref, other_ref, rem_ref)
    tri = triangles(128)

    def body(z, carry):
        for half, ref in enumerate((mine_ref, other_ref)):
            _, _, pooled = look_up(*tables, *masks(ref[z, feats + side], side, tri))
            bag_ref[half, z] = pooled.T.astype(bf16)
        return carry

    lax.fori_loop(0, zs, body, 0, unroll=2)


def feature_pool(where, mine, other, remainder):
    return pl.pallas_call(
        feature_kernel,
        in_specs=[smem] + [vmem] * 3,
        out_specs=vmem,
        out_shape=jax.ShapeDtypeStruct((2, mine.shape[0], 128, 128), bf16),
        compiler_params=PARAMS,
        cost_estimate=cost(6),
        name="feature_pool",
    )(where, mine, other, remainder)


def back_kernel(got_ref, pre_ref, out_ref, held):
    for d in range(got_ref.shape[0]):
        held[4 * d : 4 * d + 4] = got_ref[d].astype(f32)
    pre = pre_ref[...]
    sigma = jax.nn.sigmoid(pre)
    pre_grad = (held[...] * sigma * (1.0 + pre * (1.0 - sigma))).astype(bf16)
    for d in range(out_ref.shape[0]):
        out_ref[d] = pre_grad


def tower_back(got, pre, copies):
    return pl.pallas_call(
        back_kernel,
        out_shape=jax.ShapeDtypeStruct((copies, *pre.shape), bf16),
        scratch_shapes=[pltpu.VMEM(pre.shape, f32)],
        compiler_params=PARAMS,
        cost_estimate=cost(1),
        name="tower_back",
    )(got, pre)


def weight_kernel(bag_ref, mine_ref, other_ref, out_ref):
    total = jnp.zeros(out_ref.shape[1:], f32)
    for z in range(mine_ref.shape[0]):
        total += mm(bag_ref[0, z], mine_ref[z]) + mm(bag_ref[1, z], other_ref[z])
    chunk = total.astype(bf16)
    for d in range(out_ref.shape[0]):
        out_ref[d] = chunk


def weight_part(bag_t, mine, other):
    return pl.pallas_call(
        weight_kernel,
        out_shape=jax.ShapeDtypeStruct((mine.shape[0], 128, 256), bf16),
        compiler_params=PARAMS,
        cost_estimate=cost(1),
        name="weight_part",
    )(bag_t, mine, other)


def rows_kernel(where_ref, grad_mine_ref, grad_other_ref, weight_ref, mine_ref, other_ref, rem_ref, out_ref):
    feats, zs = rem_ref.shape[0], mine_ref.shape[0]
    own, side = where_ref[0], where_ref[1]
    weight = weight_ref[0, pl.ds(pl.multiple_of(own * 128, 128), 128), :]
    quot_t, rem_t = own_tables(own, mine_ref, other_ref, rem_ref)
    tri = triangles(128)

    def body(z, carry):
        quot_sum, rem_sum = carry
        for ref, got in ((grad_mine_ref, mine_ref), (grad_other_ref, other_ref)):
            quot_hot, rem_hot, member = masks(got[z, feats + side], side, tri)
            look = mm(mm_nt(weight, ref[z]).astype(bf16), member)
            quot_part = (look * mm(rem_t, rem_hot)).astype(bf16)
            rem_part = (look * mm(quot_t, quot_hot)).astype(bf16)
            quot_sum += mm_nt(quot_part, quot_hot)
            rem_sum += mm_nt(rem_part, rem_hot)
        return quot_sum, rem_sum

    start = jnp.zeros((128, 256), f32), jnp.zeros((128, 128), f32)
    quot_sum, rem_sum = lax.fori_loop(0, zs, body, start, unroll=2)
    quot_sum, rem_sum = quot_sum.T, rem_sum.T
    for z in range(zs):
        near = quot_sum[16 * z : 16 * z + 16]
        far = quot_sum[128 + 16 * z : 144 + 16 * z]
        out_ref[2 * z, :16] = jnp.where(side == 0, near, far)
        out_ref[2 * z + 1, :16] = jnp.where(side == 0, far, near)
    for d in range(2 * zs):
        out_ref[d, 16:] = rem_sum[8 * d : 8 * d + 8]


def rows_part(where, grad_mine, grad_other, weight, mine, other, remainder):
    return pl.pallas_call(
        rows_kernel,
        in_specs=[smem] + [vmem] * 6,
        out_specs=vmem,
        out_shape=jax.ShapeDtypeStruct((2 * mine.shape[0], 24, 128), f32),
        compiler_params=PARAMS,
        cost_estimate=cost(8),
        name="rows_part",
    )(where, grad_mine, grad_other, weight, mine, other, remainder)


def widen_kernel(side_ref, mine_ref, other_ref, out_ref):
    side = side_ref[0]
    for z in range(mine_ref.shape[0]):
        out_ref[z, side] = mine_ref[z].astype(f32)
        out_ref[z, 1 - side] = other_ref[z].astype(f32)


def widen(side, mine, other):
    zs, step = mine.shape[0], 2
    block = pl.BlockSpec((step, 128, 256), lambda i: (i, 0, 0))
    return pl.pallas_call(
        widen_kernel,
        grid=(zs // step,),
        in_specs=[smem, block, block],
        out_specs=pl.BlockSpec((step, 2, 128, 256), lambda i: (i, 0, 0, 0)),
        out_shape=jax.ShapeDtypeStruct((zs, 2, 128, 256), f32),
        compiler_params=PARAMS,
        cost_estimate=cost(1),
        name="widen",
    )(side, mine, other)


def on_device(
    quotient_rows,
    remainder_rows,
    quotient_index,
    remainder_index,
    bag_sizes,
    tower_weight,
    norm_gain,
    cotangent,
):
    feats = quotient_rows.shape[0]
    shards, towers = lax.axis_size("shard"), lax.axis_size("tower")
    shard = lax.axis_index("shard")
    zs = shards // 2
    along_z = [[2 * z + c for z in range(zs)] for c in range(2)]
    across = [(i, i ^ 1) for i in range(shards)]
    swap = functools.partial(lax.all_to_all, split_axis=0, concat_axis=0, tiled=True)
    gather_z = functools.partial(swap, axis_name="shard", axis_index_groups=along_z)
    side = (shard & 1).astype(jnp.int32)
    side_arg = side[None]
    where = jnp.stack([shard.astype(jnp.int32), side])
    gain = norm_gain.astype(f32)[None]

    packed, picks = pack(quotient_rows, quotient_index, remainder_index, bag_sizes)
    mine = gather_z(packed)
    other = lax.ppermute(mine, "shard", across)
    pre, act = tower_forward(side_arg, mine, other, remainder_rows, picks, tower_weight, towers)
    joint, joint_grad = norm(swap(act, "tower"), cotangent, gain)
    grad_copies = tower_back(swap(joint_grad, "tower"), pre, zs)
    bag_t = feature_pool(where, mine, other, remainder_rows)
    grad_mine, bag_t = lax.optimization_barrier((gather_z(grad_copies), bag_t))
    grad_other = lax.ppermute(grad_mine, "shard", across)

    chunk_copies = weight_part(bag_t, grad_mine, grad_other)
    rows = rows_part(where, grad_mine, grad_other, tower_weight, mine, other, remainder_rows)
    chunks_mine, rows = lax.optimization_barrier((gather_z(chunk_copies), rows))
    owned = swap(rows, "shard")
    chunks_other = lax.ppermute(chunks_mine, "shard", across)
    weight_grad = widen(side_arg, chunks_mine, chunks_other).reshape(1, feats * 128, 256)
    owned, weight_grad = lax.optimization_barrier((owned, weight_grad))
    return joint, weight_grad, owned[:, :16], owned[:, 16:]


def solution(mesh):
    in_specs = (
        P("tower", "shard", None),
        P("tower", None, None),
        P("tower", "shard", None),
        P("tower", "shard", None),
        P("tower", "shard", None),
        P("tower", None, None),
        P(),
        P("shard", "tower", None),
    )
    out_specs = (
        P("shard", "tower", None),
        P("tower", None, None),
        P("tower", "shard", None),
        P("tower", "shard", None),
    )
    return jax.shard_map(
        on_device, mesh=mesh, in_specs=in_specs, out_specs=out_specs, check_vma=False
    )
```

```python
import functools

import jax
import jax.numpy as jnp
from jax import lax
from jax.experimental import pallas as pl
from jax.experimental.pallas import tpu as pltpu
from jax.sharding import PartitionSpec as P

norm_eps = 1e-05
f32, bf16 = jnp.float32, jnp.bfloat16
NT = (((1,), (1,)), ((), ()))
PARAMS = pltpu.CompilerParams(vmem_limit_bytes=20 * 1024 * 1024)
vmem = pl.BlockSpec(memory_space=pltpu.VMEM)
smem = pl.BlockSpec(memory_space=pltpu.SMEM)
hbm = pl.BlockSpec(memory_space=pltpu.HBM)


def in_hbm(*arrays):
    return tuple(pltpu.with_memory_space_constraint(a, pltpu.HBM) for a in arrays)


def mm(a, b):
    return jnp.dot(a, b, preferred_element_type=f32)


def mm_nt(a, b):
    return lax.dot_general(a, b, NT, preferred_element_type=f32)


def cost(micros):
    return pl.CostEstimate(
        flops=int(micros * 1e8), bytes_accessed=int(micros * 3e6), transcendentals=0
    )


def triangles(n):
    row = lax.broadcasted_iota(jnp.int32, (n, n), 0)
    col = lax.broadcasted_iota(jnp.int32, (n, n), 1)
    upto = jnp.where(col <= row, 1.0, 0.0).astype(bf16)
    before = jnp.where(col < row, 1.0, 0.0).astype(bf16)
    return jnp.concatenate([upto, before], axis=0)


def masks(picks, side, tri):
    values = picks.astype(jnp.int32)
    row_q = lax.broadcasted_iota(jnp.int32, (256, 128), 0)
    row_r = lax.broadcasted_iota(jnp.int32, (128, 128), 0)
    lane = lax.broadcasted_iota(jnp.int32, (128, 128), 1).astype(f32)
    place = ((((values >> 4) & 1) ^ side) << 7) + ((values >> 5) << 4) + (values & 15)
    sums = mm_nt(tri, picks)
    ends = jnp.broadcast_to(sums[:128, 8:9], (128, 128))
    starts = jnp.broadcast_to(sums[128:, 8:9], (128, 128))
    quot, rem, member = [], [], []
    for c in range(4):
        quot.append(jnp.where(row_q == place[c : c + 1], 1.0, 0.0).astype(bf16))
        rem.append(jnp.where(row_r == values[4 + c : 5 + c], 1.0, 0.0).astype(bf16))
        here = lane + float(128 * c)
        inside = (here < ends) & (here >= starts)
        member.append(jnp.where(inside, 1.0, 0.0).astype(bf16))
    return tuple(jnp.concatenate(v, axis=1) for v in (quot, rem, member))


def look_up(quot_t, rem_t, quot_hot, rem_hot, member):
    quot = mm(quot_t, quot_hot)
    rem = mm(rem_t, rem_hot)
    composed = quot * rem
    high = composed.astype(bf16)
    low = (composed - high.astype(f32)).astype(bf16)
    return quot, rem, mm_nt(member, high) + mm_nt(member, low)


def pack_kernel(rows_ref, quot_ref, rem_ref, size_ref, out_ref, picks_ref, held):
    feats = rows_ref.shape[0]
    held[...] = jnp.zeros_like(held)
    for f in range(feats):
        for c in range(4):
            part = pl.ds(128 * c, 128)
            held[f, c : c + 1, :] = quot_ref[f, :, part].astype(f32)
            held[f, 4 + c : 5 + c, :] = rem_ref[f, :, part].astype(f32)
        held[f, 8:9, :] = size_ref[f].astype(f32)
    picks = held[...].astype(bf16)
    picks_ref[...] = picks
    rows = rows_ref[...]
    for z in range(out_ref.shape[0]):
        out_ref[z, :feats] = rows
        out_ref[z, feats:] = picks[2 * z : 2 * z + 2]


def pack(rows, quot, rem, sizes):
    feats, zs = rows.shape[0], rows.shape[0] // 2
    whole = lambda a: pl.BlockSpec(a.shape, lambda i: (0, 0, 0))
    pinned = in_hbm(rows, quot, rem, sizes)
    return pl.pallas_call(
        pack_kernel,
        grid=(1,),
        in_specs=[whole(a) for a in pinned],
        out_specs=[
            pl.BlockSpec((zs, feats + 2, 16, 128), lambda i: (0, 0, 0, 0)),
            pl.BlockSpec((feats, 16, 128), lambda i: (0, 0, 0)),
        ],
        out_shape=[
            jax.ShapeDtypeStruct((zs, feats + 2, 16, 128), bf16),
            jax.ShapeDtypeStruct((feats, 16, 128), bf16),
        ],
        scratch_shapes=[pltpu.VMEM((feats, 16, 128), f32)],
        compiler_params=PARAMS,
        cost_estimate=cost(1),
        name="pack",
    )(*pinned)


def tower_kernel(side_ref, mine_ref, other_ref, rem_ref, picks_ref, weight_ref, pre_ref):
    tri = triangles(128)
    side = side_ref[0]
    bags = []
    for f in range(rem_ref.shape[0]):
        table = jnp.concatenate(
            [mine_ref[:, f].reshape(128, 128), other_ref[:, f].reshape(128, 128)], axis=0
        )
        _, _, pooled = look_up(table.T, rem_ref[f].T, *masks(picks_ref[f], side, tri))
        bags.append(pooled.astype(bf16))
    pre_ref[...] = mm(jnp.concatenate(bags, axis=1), weight_ref[0])


def tower_forward(side, mine, other, remainder, picks, weight):
    return pl.pallas_call(
        tower_kernel,
        in_specs=[smem] + [vmem] * 5,
        out_specs=vmem,
        out_shape=jax.ShapeDtypeStruct((128, 256), f32),
        compiler_params=PARAMS,
        cost_estimate=cost(6),
        name="tower_forward",
    )(side, mine, other, remainder, picks, weight)


def silu(pre):
    return (pre * jax.nn.sigmoid(pre)).astype(bf16).astype(f32)


def stats_kernel(pre_ref, cot_ref, gain_ref, out_ref, scaled_ref):
    act = silu(pre_ref[...])
    for d in range(cot_ref.shape[0]):
        scaled_ref[4 * d : 4 * d + 4] = cot_ref[d].astype(f32) * gain_ref[...]
    mean = jnp.mean(act, axis=1, keepdims=True)
    center = act - mean
    scaled = scaled_ref[...]
    spread = jnp.sum(center * center, axis=1, keepdims=True)
    total = jnp.sum(scaled, axis=1, keepdims=True)
    lean = jnp.sum(scaled * center, axis=1, keepdims=True)
    lane = lax.broadcasted_iota(jnp.int32, (128, 128), 1)
    table = jnp.where(
        lane == 0, mean, jnp.where(lane == 1, spread, jnp.where(lane == 2, total, lean))
    )
    stats = table.T[:4]
    for d in range(out_ref.shape[0]):
        rows = act[4 * d : 4 * d + 4]
        out_ref[d, 0], out_ref[d, 1], out_ref[d, 2] = rows[:, :128], rows[:, 128:], stats


def local_stats(pre, cot, gain, towers):
    return pl.pallas_call(
        stats_kernel,
        out_shape=[
            jax.ShapeDtypeStruct((towers, 3, 4, 128), f32),
            jax.ShapeDtypeStruct(pre.shape, f32),
        ],
        compiler_params=PARAMS,
        cost_estimate=cost(1),
        name="local_stats",
    )(pre, cot, gain)


def norm_kernel(got_ref, gain_ref, joint_ref):
    towers = got_ref.shape[0]
    columns = float(towers * 256)
    pieces = [(t, h, pl.ds(256 * t + 128 * h, 128)) for t in range(towers) for h in range(2)]
    mean = sum(got_ref[t, h] for t, h, _ in pieces)
    mean = jnp.sum(mean, axis=1, keepdims=True) * (1.0 / columns)
    center = [got_ref[t, h] - mean for t, h, _ in pieces]
    spread = jnp.sum(sum(c * c for c in center), axis=1, keepdims=True) * (1.0 / columns)
    scale = lax.rsqrt(spread + norm_eps)
    for c, (_, _, part) in zip(center, pieces):
        joint_ref[0, :, part] = (c * scale * gain_ref[:, part]).astype(bf16)


def norm(got, gain):
    return pl.pallas_call(
        norm_kernel,
        out_shape=jax.ShapeDtypeStruct((1, 4, gain.shape[1]), bf16),
        compiler_params=PARAMS,
        cost_estimate=cost(1),
        name="norm",
    )(got, gain)


def feature_kernel(per_step, where_ref, mine_ref, other_ref, rem_ref, picks_ref, *refs):
    bag_ref, quot_ref, remd_ref, qhot_ref, rhot_ref, member_ref, qt_ref, rt_ref = refs

    @pl.when((pl.program_id(0) == 0) & (pl.program_id(1) == 0))
    def _():
        qt_ref[:, :128] = mine_ref[:, 0].reshape(128, 128).T
        qt_ref[:, 128:] = other_ref[:, 0].reshape(128, 128).T
        rt_ref[...] = rem_ref[0].T

    tri = triangles(128)
    for i in range(per_step):
        hot = masks(picks_ref[0, i], where_ref[1], tri)
        quot, rem, pooled = look_up(qt_ref[...], rt_ref[...], *hot)
        bag_ref[0, i] = pooled.T.astype(bf16)
        quot_ref[0, i], remd_ref[0, i] = quot.astype(bf16), rem.astype(bf16)
        qhot_ref[0, i], rhot_ref[0, i], member_ref[0, i] = hot


def step_block(per_step, *dims):
    return pl.BlockSpec((1, per_step, *dims), lambda h, i, w: (h, i, 0, 0))


def feature_pool(where, mine, other, remainder, picks):
    zs, per_step = picks.shape[1], 4
    table = pl.BlockSpec((zs, 1, 16, 128), lambda h, i, w: (0, w[0], 0, 0))
    sizes = [(128, 128), (128, 512), (128, 512), (256, 512), (128, 512), (128, 512)]
    return pl.pallas_call(
        functools.partial(feature_kernel, per_step),
        grid_spec=pltpu.PrefetchScalarGridSpec(
            num_scalar_prefetch=1,
            grid=(2, zs // per_step),
            in_specs=[
                table,
                table,
                pl.BlockSpec((1, 128, 128), lambda h, i, w: (w[0], 0, 0)),
                step_block(per_step, 16, 128),
            ],
            out_specs=[step_block(per_step, *s) for s in sizes],
            scratch_shapes=[pltpu.VMEM((128, 256), bf16), pltpu.VMEM((128, 128), bf16)],
        ),
        out_shape=[pltpu.HBM((2, zs, *s), bf16) for s in sizes],
        compiler_params=PARAMS,
        cost_estimate=cost(6),
        name="feature_pool",
    )(where, mine, other, *in_hbm(remainder), picks)


def back_kernel(columns, got_ref, pre_ref, scaled_ref, out_ref):
    towers = got_ref.shape[0]
    stats = got_ref[:, 2]
    sums = jnp.sum(stats, axis=0)
    mean = sums[0:1] * (1.0 / towers)
    shift = stats[:, 0:1, :] - mean[None]
    spread = sums[1:2] + (columns / towers) * jnp.sum(shift * shift, axis=0)
    lean = sums[3:4] + jnp.sum(stats[:, 2:3, :] * shift, axis=0)
    scale = lax.rsqrt(spread * (1.0 / columns) + norm_eps)
    rows = [mean, scale, sums[2:3] * (1.0 / columns), lean * scale * scale * (1.0 / columns)]
    table = jnp.concatenate(rows + [jnp.zeros((124, 128), f32)], axis=0).T
    mean, scale, total, lean = (table[:, i : i + 1] for i in range(4))
    pre = pre_ref[...]
    sigma = jax.nn.sigmoid(pre)
    grad = (scale * (scaled_ref[...] - total - (silu(pre) - mean) * lean)).astype(bf16).astype(f32)
    pre_grad = (grad * sigma * (1.0 + pre * (1.0 - sigma))).astype(bf16)
    for d in range(out_ref.shape[0]):
        out_ref[d] = pre_grad


def tower_back(got, pre, scaled, copies):
    columns = got.shape[0] * pre.shape[1]
    return pl.pallas_call(
        functools.partial(back_kernel, float(columns)),
        out_shape=jax.ShapeDtypeStruct((copies, *pre.shape), bf16),
        compiler_params=PARAMS,
        cost_estimate=cost(1),
        name="tower_back",
    )(got, pre, scaled)


def grads_kernel(per_step, where_ref, mine_ref, other_ref, weight_ref, *refs):
    bag_ref, quot_ref, remd_ref, qhot_ref, rhot_ref, member_ref, out_ref, wg_ref, qg_ref, rg_ref = refs
    half, step = pl.program_id(0), pl.program_id(1)

    @pl.when((half == 0) & (step == 0))
    def _():
        wg_ref[...] = jnp.zeros_like(wg_ref)
        qg_ref[...] = jnp.zeros_like(qg_ref)
        rg_ref[...] = jnp.zeros_like(rg_ref)

    weight_sum, quot_sum, rem_sum = wg_ref[...], qg_ref[...], rg_ref[...]
    for i in range(per_step):
        grad = jnp.where(half == 0, mine_ref[i], other_ref[i])
        weight_sum += mm(bag_ref[0, i], grad)
        look = mm(mm_nt(weight_ref[0], grad).astype(bf16), member_ref[0, i])
        quot_part = (look * remd_ref[0, i].astype(f32)).astype(bf16)
        rem_part = (look * quot_ref[0, i].astype(f32)).astype(bf16)
        quot_sum += mm_nt(quot_part, qhot_ref[0, i])
        rem_sum += mm_nt(rem_part, rhot_ref[0, i])
    wg_ref[...], qg_ref[...], rg_ref[...] = weight_sum, quot_sum, rem_sum

    @pl.when((half == pl.num_programs(0) - 1) & (step == pl.num_programs(1) - 1))
    def _():
        side = where_ref[1]
        chunk = weight_sum.astype(bf16)
        quot, rem = quot_sum.T, rem_sum.T
        for z in range(out_ref.shape[0]):
            near, far = quot[16 * z : 16 * z + 16], quot[128 + 16 * z : 144 + 16 * z]
            first, second = jnp.where(side == 0, near, far), jnp.where(side == 0, far, near)
            pair = jnp.concatenate([rem[16 * z : 16 * z + 8], rem[16 * z + 8 : 16 * z + 16]], axis=1)
            out_ref[z, :128] = chunk
            out_ref[z, 128:144] = jnp.concatenate([first, second], axis=1).astype(bf16)
            out_ref[z, 144:160] = jnp.concatenate([pair, jnp.zeros_like(pair)], axis=0).astype(bf16)


def grads_part(where, mine, other, weight, *looked):
    zs, per_step = mine.shape[0], 4
    grads = pl.BlockSpec((per_step, 128, 256), lambda h, i, w: (i, 0, 0))
    return pl.pallas_call(
        functools.partial(grads_kernel, per_step),
        grid_spec=pltpu.PrefetchScalarGridSpec(
            num_scalar_prefetch=1,
            grid=(2, zs // per_step),
            in_specs=[grads, grads, pl.BlockSpec((1, 128, 256), lambda h, i, w: (0, w[0], 0))]
            + [step_block(per_step, *a.shape[2:]) for a in looked],
            out_specs=pl.BlockSpec((zs, 160, 256), lambda h, i, w: (0, 0, 0)),
            scratch_shapes=[
                pltpu.VMEM((128, 256), f32),
                pltpu.VMEM((128, 256), f32),
                pltpu.VMEM((128, 128), f32),
            ],
        ),
        out_shape=jax.ShapeDtypeStruct((zs, 160, 256), bf16),
        compiler_params=PARAMS,
        cost_estimate=cost(8),
        name="grads_part",
    )(where, mine, other, *in_hbm(weight, *looked))


def spread_kernel(side_ref, mine_ref, other_ref, weight_ref, quot_ref, rem_ref):
    side = side_ref[0]
    for z in range(mine_ref.shape[0]):
        for at, ref in ((side, mine_ref), (1 - side, other_ref)):
            weight_ref[z, at] = ref[z, :128].astype(f32)
            rows = ref[z, 128:160].astype(f32)
            rows = jnp.where(side == 0, rows[:, :128], rows[:, 128:])
            quot_ref[z, at] = rows[:16]
            rem_ref[z, at] = rows[16:24]


def spread(side, mine, other):
    zs, step = mine.shape[0], 2
    block = pl.BlockSpec((step, 160, 256), lambda i: (i, 0, 0))
    sizes = [(128, 256), (16, 128), (8, 128)]
    return pl.pallas_call(
        spread_kernel,
        grid=(zs // step,),
        in_specs=[smem, block, block],
        out_specs=[pl.BlockSpec((step, 2, *s), lambda i: (i, 0, 0, 0)) for s in sizes],
        out_shape=[jax.ShapeDtypeStruct((zs, 2, *s), f32) for s in sizes],
        compiler_params=PARAMS,
        cost_estimate=cost(2),
        name="spread",
    )(side, mine, other)


def on_device(
    quotient_rows,
    remainder_rows,
    quotient_index,
    remainder_index,
    bag_sizes,
    tower_weight,
    norm_gain,
    cotangent,
):
    feats = quotient_rows.shape[0]
    shards, towers = lax.axis_size("shard"), lax.axis_size("tower")
    shard, tower = lax.axis_index("shard"), lax.axis_index("tower")
    zs = shards // 2
    along_z = [[2 * z + c for z in range(zs)] for c in range(2)]
    across = [(i, i ^ 1) for i in range(shards)]
    swap = functools.partial(lax.all_to_all, split_axis=0, concat_axis=0, tiled=True)
    gather_z = functools.partial(swap, axis_name="shard", axis_index_groups=along_z)
    side = (shard & 1).astype(jnp.int32)
    side_arg = side[None]
    where = jnp.stack([shard.astype(jnp.int32), side])
    gain = norm_gain.astype(f32)[None]

    gain_here = lax.dynamic_slice(norm_gain, (tower * 256,), (256,)).astype(f32)[None]

    packed, picks = pack(quotient_rows, quotient_index, remainder_index, bag_sizes)
    mine, late = lax.optimization_barrier((gather_z(packed), cotangent[0]))
    other = lax.ppermute(mine, "shard", across)
    late = late.reshape(4, towers, 256).transpose(1, 0, 2)
    pre = tower_forward(side_arg, mine, other, remainder_rows, picks, tower_weight)
    pre, cot = lax.optimization_barrier((pre, swap(late, "tower")))
    sent, scaled = local_stats(pre, cot, gain_here, towers)
    stats = swap(sent, "tower")
    grad_copies = tower_back(stats, pre, scaled, zs)
    joint = norm(stats, gain)
    all_picks = lax.dynamic_index_in_dim(
        jnp.stack([mine[:, feats:], other[:, feats:]]), side, 2, keepdims=False
    )
    looked = feature_pool(where, mine, other, remainder_rows, all_picks)
    grad_mine, joint, *looked = lax.optimization_barrier((gather_z(grad_copies), joint, *looked))
    grad_other = lax.ppermute(grad_mine, "shard", across)
    got_mine = gather_z(grads_part(where, grad_mine, grad_other, tower_weight, *looked))
    got_other = lax.ppermute(got_mine, "shard", across)
    weight_grad, quot_grad, rem_grad = spread(side_arg, got_mine, got_other)
    return (
        joint,
        weight_grad.reshape(1, feats * 128, 256),
        quot_grad.reshape(feats, 16, 128),
        rem_grad.reshape(feats, 8, 128),
    )


def solution(mesh):
    in_specs = (
        P("tower", "shard", None),
        P("tower", None, None),
        P("tower", "shard", None),
        P("tower", "shard", None),
        P("tower", "shard", None),
        P("tower", None, None),
        P(),
        P("shard", "tower", None),
    )
    out_specs = (
        P("shard", "tower", None),
        P("tower", None, None),
        P("tower", "shard", None),
        P("tower", "shard", None),
    )
    return jax.shard_map(
        on_device, mesh=mesh, in_specs=in_specs, out_specs=out_specs, check_vma=False
    )
```

```python
import functools

import jax
import jax.numpy as jnp
from jax import lax
from jax.experimental import pallas as pl
from jax.experimental.pallas import tpu as pltpu
from jax.sharding import PartitionSpec as P

norm_eps = 1e-05
f32, bf16 = jnp.float32, jnp.bfloat16
NT = (((1,), (1,)), ((), ()))
PARAMS = pltpu.CompilerParams(vmem_limit_bytes=20 * 1024 * 1024)
vmem = pl.BlockSpec(memory_space=pltpu.VMEM)
smem = pl.BlockSpec(memory_space=pltpu.SMEM)
hbm = pl.BlockSpec(memory_space=pltpu.HBM)


def in_hbm(*arrays):
    return tuple(pltpu.with_memory_space_constraint(a, pltpu.HBM) for a in arrays)


def in_vmem(*arrays):
    return tuple(pltpu.with_memory_space_constraint(a, pltpu.VMEM) for a in arrays)


def mm(a, b):
    return jnp.dot(a, b, preferred_element_type=f32)


def mm_nt(a, b):
    return lax.dot_general(a, b, NT, preferred_element_type=f32)


def cost(micros):
    return pl.CostEstimate(
        flops=int(micros * 1e8), bytes_accessed=int(micros * 3e6), transcendentals=0
    )


def triangles(n):
    row = lax.broadcasted_iota(jnp.int32, (n, n), 0)
    col = lax.broadcasted_iota(jnp.int32, (n, n), 1)
    upto = jnp.where(col <= row, 1.0, 0.0).astype(bf16)
    before = jnp.where(col < row, 1.0, 0.0).astype(bf16)
    return jnp.concatenate([upto, before], axis=0)


def masks(picks, side, tri):
    values = picks.astype(jnp.int32)
    row_q = lax.broadcasted_iota(jnp.int32, (256, 128), 0)
    row_r = lax.broadcasted_iota(jnp.int32, (128, 128), 0)
    lane = lax.broadcasted_iota(jnp.int32, (128, 128), 1).astype(f32)
    place = ((((values >> 4) & 1) ^ side) << 7) + ((values >> 5) << 4) + (values & 15)
    sums = mm_nt(tri, picks)
    ends = jnp.broadcast_to(sums[:128, 8:9], (128, 128))
    starts = jnp.broadcast_to(sums[128:, 8:9], (128, 128))
    quot, rem, member = [], [], []
    for c in range(4):
        quot.append(jnp.where(row_q == place[c : c + 1], 1.0, 0.0).astype(bf16))
        rem.append(jnp.where(row_r == values[4 + c : 5 + c], 1.0, 0.0).astype(bf16))
        here = lane + float(128 * c)
        inside = (here < ends) & (here >= starts)
        member.append(jnp.where(inside, 1.0, 0.0).astype(bf16))
    return tuple(jnp.concatenate(v, axis=1) for v in (quot, rem, member))


def look_up(quot_t, rem_t, quot_hot, rem_hot, member):
    quot = mm(quot_t, quot_hot)
    rem = mm(rem_t, rem_hot)
    composed = quot * rem
    high = composed.astype(bf16)
    low = (composed - high.astype(f32)).astype(bf16)
    return quot, rem, mm_nt(member, high) + mm_nt(member, low)


def pack_kernel(rows_ref, quot_ref, rem_ref, size_ref, out_ref, picks_ref, held):
    feats = rows_ref.shape[0]
    held[...] = jnp.zeros_like(held)
    for f in range(feats):
        for c in range(4):
            part = pl.ds(128 * c, 128)
            held[f, c : c + 1, :] = quot_ref[f, :, part].astype(f32)
            held[f, 4 + c : 5 + c, :] = rem_ref[f, :, part].astype(f32)
        held[f, 8:9, :] = size_ref[f].astype(f32)
    picks = held[...].astype(bf16)
    picks_ref[...] = picks
    rows = rows_ref[...]
    for z in range(out_ref.shape[0]):
        out_ref[z, :feats] = rows
        out_ref[z, feats:] = picks[2 * z : 2 * z + 2]


def pack(rows, quot, rem, sizes):
    feats, zs = rows.shape[0], rows.shape[0] // 2
    whole = lambda a: pl.BlockSpec(a.shape, lambda i: (0, 0, 0))
    pinned = in_hbm(rows, quot, rem, sizes)
    return pl.pallas_call(
        pack_kernel,
        grid=(1,),
        in_specs=[whole(a) for a in pinned],
        out_specs=[
            pl.BlockSpec((zs, feats + 2, 16, 128), lambda i: (0, 0, 0, 0)),
            pl.BlockSpec((feats, 16, 128), lambda i: (0, 0, 0)),
        ],
        out_shape=[
            jax.ShapeDtypeStruct((zs, feats + 2, 16, 128), bf16),
            jax.ShapeDtypeStruct((feats, 16, 128), bf16),
        ],
        scratch_shapes=[pltpu.VMEM((feats, 16, 128), f32)],
        compiler_params=PARAMS,
        cost_estimate=cost(1),
        name="pack",
    )(*pinned)


def tower_kernel(side_ref, mine_ref, other_ref, rem_ref, picks_ref, weight_ref, pre_ref):
    tri = triangles(128)
    side = side_ref[0]
    bags = []
    for f in range(rem_ref.shape[0]):
        table = jnp.concatenate(
            [mine_ref[:, f].reshape(128, 128), other_ref[:, f].reshape(128, 128)], axis=0
        )
        _, _, pooled = look_up(table.T, rem_ref[f].T, *masks(picks_ref[f], side, tri))
        bags.append(pooled.astype(bf16))
    pre_ref[...] = mm(jnp.concatenate(bags, axis=1), weight_ref[0])


def tower_forward(side, mine, other, remainder, picks, weight):
    return pl.pallas_call(
        tower_kernel,
        in_specs=[smem] + [vmem] * 5,
        out_specs=vmem,
        out_shape=jax.ShapeDtypeStruct((128, 256), f32),
        compiler_params=PARAMS,
        cost_estimate=cost(6),
        name="tower_forward",
    )(side, mine, other, remainder, picks, weight)


def silu(pre):
    return (pre * jax.nn.sigmoid(pre)).astype(bf16).astype(f32)


def stats_kernel(where_ref, pre_ref, cot_ref, gain_ref, out_ref, scaled_ref):
    act = silu(pre_ref[...])
    gain = gain_ref[:, pl.ds(pl.multiple_of(where_ref[2] * 256, 256), 256)]
    for d in range(cot_ref.shape[0]):
        scaled_ref[4 * d : 4 * d + 4] = cot_ref[d].astype(f32) * gain
    mean = jnp.mean(act, axis=1, keepdims=True)
    center = act - mean
    scaled = scaled_ref[...]
    spread = jnp.sum(center * center, axis=1, keepdims=True)
    total = jnp.sum(scaled, axis=1, keepdims=True)
    lean = jnp.sum(scaled * center, axis=1, keepdims=True)
    lane = lax.broadcasted_iota(jnp.int32, (128, 128), 1)
    table = jnp.where(
        lane == 0, mean, jnp.where(lane == 1, spread, jnp.where(lane == 2, total, lean))
    )
    stats = table.T[:4]
    for d in range(out_ref.shape[0]):
        rows = act[4 * d : 4 * d + 4]
        out_ref[d, 0], out_ref[d, 1], out_ref[d, 2] = rows[:, :128], rows[:, 128:], stats


def local_stats(where, pre, cot, gain, towers):
    return pl.pallas_call(
        stats_kernel,
        in_specs=[smem] + [vmem] * 3,
        out_specs=[vmem] * 2,
        out_shape=[
            jax.ShapeDtypeStruct((towers, 3, 4, 128), f32),
            jax.ShapeDtypeStruct(pre.shape, f32),
        ],
        compiler_params=PARAMS,
        cost_estimate=cost(1),
        name="local_stats",
    )(where, pre, cot, gain)


def norm_kernel(got_ref, gain_ref, joint_ref):
    towers = got_ref.shape[0]
    columns = float(towers * 256)
    pieces = [(t, h, pl.ds(256 * t + 128 * h, 128)) for t in range(towers) for h in range(2)]
    mean = sum(got_ref[t, h] for t, h, _ in pieces)
    mean = jnp.sum(mean, axis=1, keepdims=True) * (1.0 / columns)
    center = [got_ref[t, h] - mean for t, h, _ in pieces]
    spread = jnp.sum(sum(c * c for c in center), axis=1, keepdims=True) * (1.0 / columns)
    scale = lax.rsqrt(spread + norm_eps)
    for c, (_, _, part) in zip(center, pieces):
        joint_ref[0, :, part] = (c * scale * gain_ref[:, part]).astype(bf16)


def norm(got, gain):
    return pl.pallas_call(
        norm_kernel,
        out_shape=jax.ShapeDtypeStruct((1, 4, gain.shape[1]), bf16),
        compiler_params=PARAMS,
        cost_estimate=cost(1),
        name="norm",
    )(got, gain)


def feature_kernel(per_step, where_ref, mine_ref, other_ref, rem_ref, picks_ref, *refs):
    bag_ref, quot_ref, remd_ref, qhot_ref, rhot_ref, member_ref, qt_ref, rt_ref = refs

    @pl.when((pl.program_id(0) == 0) & (pl.program_id(1) == 0))
    def _():
        qt_ref[:, :128] = mine_ref[:, 0].reshape(128, 128).T
        qt_ref[:, 128:] = other_ref[:, 0].reshape(128, 128).T
        rt_ref[...] = rem_ref[0].T

    tri = triangles(128)
    for i in range(per_step):
        hot = masks(picks_ref[0, i], where_ref[1], tri)
        quot, rem, pooled = look_up(qt_ref[...], rt_ref[...], *hot)
        bag_ref[0, i] = pooled.T.astype(bf16)
        quot_ref[0, i], remd_ref[0, i] = quot.astype(bf16), rem.astype(bf16)
        qhot_ref[0, i], rhot_ref[0, i], member_ref[0, i] = hot


def step_block(per_step, *dims):
    return pl.BlockSpec((1, per_step, *dims), lambda h, i, w: (h, i, 0, 0))


def feature_pool(where, mine, other, remainder, picks):
    zs, per_step = picks.shape[1], 4
    table = pl.BlockSpec((zs, 1, 16, 128), lambda h, i, w: (0, w[0], 0, 0))
    sizes = [(128, 128), (128, 512), (128, 512), (256, 512), (128, 512), (128, 512)]
    return pl.pallas_call(
        functools.partial(feature_kernel, per_step),
        grid_spec=pltpu.PrefetchScalarGridSpec(
            num_scalar_prefetch=1,
            grid=(2, zs // per_step),
            in_specs=[
                table,
                table,
                pl.BlockSpec((1, 128, 128), lambda h, i, w: (w[0], 0, 0)),
                step_block(per_step, 16, 128),
            ],
            out_specs=[step_block(per_step, *s) for s in sizes],
            scratch_shapes=[pltpu.VMEM((128, 256), bf16), pltpu.VMEM((128, 128), bf16)],
        ),
        out_shape=[pltpu.HBM((2, zs, *s), bf16) for s in sizes],
        compiler_params=PARAMS,
        cost_estimate=cost(6),
        name="feature_pool",
    )(where, mine, other, *in_hbm(remainder), picks)


def back_kernel(columns, got_ref, pre_ref, scaled_ref, out_ref):
    towers = got_ref.shape[0]
    stats = got_ref[:, 2]
    sums = jnp.sum(stats, axis=0)
    mean = sums[0:1] * (1.0 / towers)
    shift = stats[:, 0:1, :] - mean[None]
    spread = sums[1:2] + (columns / towers) * jnp.sum(shift * shift, axis=0)
    lean = sums[3:4] + jnp.sum(stats[:, 2:3, :] * shift, axis=0)
    scale = lax.rsqrt(spread * (1.0 / columns) + norm_eps)
    rows = [mean, scale, sums[2:3] * (1.0 / columns), lean * scale * scale * (1.0 / columns)]
    table = jnp.concatenate(rows + [jnp.zeros((124, 128), f32)], axis=0).T
    mean, scale, total, lean = (table[:, i : i + 1] for i in range(4))
    pre = pre_ref[...]
    sigma = jax.nn.sigmoid(pre)
    grad = (scale * (scaled_ref[...] - total - (silu(pre) - mean) * lean)).astype(bf16).astype(f32)
    pre_grad = (grad * sigma * (1.0 + pre * (1.0 - sigma))).astype(bf16)
    for d in range(out_ref.shape[0]):
        out_ref[d] = pre_grad


def tower_back(got, pre, scaled, copies):
    columns = got.shape[0] * pre.shape[1]
    return pl.pallas_call(
        functools.partial(back_kernel, float(columns)),
        out_shape=jax.ShapeDtypeStruct((copies, *pre.shape), bf16),
        compiler_params=PARAMS,
        cost_estimate=cost(1),
        name="tower_back",
    )(got, pre, scaled)


CUTS = ((0, 0, 2), (0, 2, 4), (0, 4, 8), (1, 0, 4), (1, 4, 8))


def grads_kernel(where_ref, mine_ref, other_ref, weight_ref, *refs):
    kept, out_ref, held, sems = refs[:6], refs[6], refs[7:13], refs[13]
    own, side = where_ref[0], where_ref[1]
    loads = []
    for c, (half, low, high) in enumerate(CUTS):
        part = pl.ds(low, high - low)
        loads.append(
            [
                pltpu.make_async_copy(a.at[half, part], b.at[half, part], sems.at[c, i])
                for i, (a, b) in enumerate(zip(kept, held))
            ]
        )
    for copies in loads:
        for copy in copies:
            copy.start()
    bags, quots, rems, quot_hot, rem_hot, member = held
    weight = weight_ref[0, pl.ds(pl.multiple_of(own * 128, 128), 128), :]
    weight_sum, quot_sum = jnp.zeros((128, 256), f32), jnp.zeros((128, 256), f32)
    rem_sum = jnp.zeros((128, 128), f32)
    for copies, (half, low, high) in zip(loads, CUTS):
        for copy in copies:
            copy.wait()
        for z in range(low, high):
            grad = (mine_ref, other_ref)[half][z]
            weight_sum += mm(bags[half, z], grad)
            look = mm(mm_nt(weight, grad).astype(bf16), member[half, z])
            quot_part = (look * rems[half, z].astype(f32)).astype(bf16)
            rem_part = (look * quots[half, z].astype(f32)).astype(bf16)
            quot_sum += mm_nt(quot_part, quot_hot[half, z])
            rem_sum += mm_nt(rem_part, rem_hot[half, z])
    chunk = weight_sum.astype(bf16)
    quot, rem = quot_sum.T, rem_sum.T
    for z in range(out_ref.shape[0]):
        near, far = quot[16 * z : 16 * z + 16], quot[128 + 16 * z : 144 + 16 * z]
        first, second = jnp.where(side == 0, near, far), jnp.where(side == 0, far, near)
        pair = jnp.concatenate([rem[16 * z : 16 * z + 8], rem[16 * z + 8 : 16 * z + 16]], axis=1)
        rows = jnp.concatenate([jnp.concatenate([first, second], axis=1), pair], axis=0)
        out_ref[z, :128] = chunk
        out_ref[z, 128:] = rows.astype(bf16)


def grads_part(where, mine, other, weight, *looked):
    return pl.pallas_call(
        grads_kernel,
        in_specs=[smem] + [vmem] * 3 + [hbm] * 6,
        out_specs=vmem,
        out_shape=jax.ShapeDtypeStruct((mine.shape[0], 152, 256), bf16),
        scratch_shapes=[pltpu.VMEM(a.shape, bf16) for a in looked]
        + [pltpu.SemaphoreType.DMA((len(CUTS), 6))],
        compiler_params=PARAMS,
        cost_estimate=cost(8),
        name="grads_part",
    )(where, mine, other, weight, *in_hbm(*looked))


def spread_kernel(side_ref, mine_ref, other_ref, weight_ref, quot_ref, rem_ref):
    side = side_ref[0]
    for z in range(mine_ref.shape[0]):
        for at, ref in ((side, mine_ref), (1 - side, other_ref)):
            weight_ref[z, at] = ref[z, :128].astype(f32)
            rows = ref[z, 128:152].astype(f32)
            rows = jnp.where(side == 0, rows[:, :128], rows[:, 128:])
            quot_ref[z, at] = rows[:16]
            rem_ref[z, at] = rows[16:]


def spread(side, mine, other):
    zs, step = mine.shape[0], 2
    block = pl.BlockSpec((step, 152, 256), lambda i: (i, 0, 0))
    sizes = [(128, 256), (16, 128), (8, 128)]
    return pl.pallas_call(
        spread_kernel,
        grid=(zs // step,),
        in_specs=[smem, block, block],
        out_specs=[pl.BlockSpec((step, 2, *s), lambda i: (i, 0, 0, 0)) for s in sizes],
        out_shape=[jax.ShapeDtypeStruct((zs, 2, *s), f32) for s in sizes],
        compiler_params=PARAMS,
        cost_estimate=cost(2),
        name="spread",
    )(side, mine, other)


def on_device(
    quotient_rows,
    remainder_rows,
    quotient_index,
    remainder_index,
    bag_sizes,
    tower_weight,
    norm_gain,
    cotangent,
):
    feats = quotient_rows.shape[0]
    shards, towers = lax.axis_size("shard"), lax.axis_size("tower")
    shard, tower = lax.axis_index("shard"), lax.axis_index("tower")
    zs = shards // 2
    along_z = [[2 * z + c for z in range(zs)] for c in range(2)]
    across = [(i, i ^ 1) for i in range(shards)]
    swap = functools.partial(lax.all_to_all, split_axis=0, concat_axis=0, tiled=True)
    gather_z = functools.partial(swap, axis_name="shard", axis_index_groups=along_z)
    side = (shard & 1).astype(jnp.int32)
    side_arg = side[None]
    where = jnp.stack([shard, side, tower]).astype(jnp.int32)
    packed, picks = pack(quotient_rows, quotient_index, remainder_index, bag_sizes)
    mine, late = lax.optimization_barrier((gather_z(packed), cotangent[0]))
    other = lax.ppermute(mine, "shard", across)
    late = late.reshape(4, towers, 256).transpose(1, 0, 2)
    pre = tower_forward(side_arg, mine, other, remainder_rows, picks, tower_weight)
    pre, norm_gain = lax.optimization_barrier((pre, norm_gain))
    gain = norm_gain.astype(f32)[None]
    pre, gain, cot = lax.optimization_barrier((pre, gain, swap(late, "tower")))
    sent, scaled = local_stats(where, pre, cot, gain, towers)
    stats = swap(sent, "tower")
    grad_copies = tower_back(stats, pre, scaled, zs)
    joint = norm(stats, gain)
    all_picks = lax.dynamic_index_in_dim(
        jnp.stack([mine[:, feats:], other[:, feats:]]), side, 2, keepdims=False
    )
    looked = feature_pool(where, mine, other, remainder_rows, all_picks)
    grad_mine, joint, *looked = lax.optimization_barrier((gather_z(grad_copies), joint, *looked))
    grad_other = lax.ppermute(grad_mine, "shard", across)
    got_mine = gather_z(grads_part(where, grad_mine, grad_other, tower_weight, *looked))
    got_other = lax.ppermute(got_mine, "shard", across)
    weight_grad, quot_grad, rem_grad = spread(side_arg, got_mine, got_other)
    return (
        joint,
        weight_grad.reshape(1, feats * 128, 256),
        quot_grad.reshape(feats, 16, 128),
        rem_grad.reshape(feats, 8, 128),
    )


def solution(mesh):
    in_specs = (
        P("tower", "shard", None),
        P("tower", None, None),
        P("tower", "shard", None),
        P("tower", "shard", None),
        P("tower", "shard", None),
        P("tower", None, None),
        P(),
        P("shard", "tower", None),
    )
    out_specs = (
        P("shard", "tower", None),
        P("tower", None, None),
        P("tower", "shard", None),
        P("tower", "shard", None),
    )
    return jax.shard_map(
        on_device, mesh=mesh, in_specs=in_specs, out_specs=out_specs, check_vma=False
    )
```

```python
import functools

import jax
import jax.numpy as jnp
from jax import lax
from jax.experimental import pallas as pl
from jax.experimental.pallas import tpu as pltpu
from jax.sharding import PartitionSpec as P

norm_eps = 1e-05
f32, bf16 = jnp.float32, jnp.bfloat16
NT = (((1,), (1,)), ((), ()))
PARAMS = pltpu.CompilerParams(vmem_limit_bytes=20 * 1024 * 1024)
vmem = pl.BlockSpec(memory_space=pltpu.VMEM)
smem = pl.BlockSpec(memory_space=pltpu.SMEM)
hbm = pl.BlockSpec(memory_space=pltpu.HBM)


def in_hbm(*arrays):
    return tuple(pltpu.with_memory_space_constraint(a, pltpu.HBM) for a in arrays)


def in_vmem(*arrays):
    return tuple(pltpu.with_memory_space_constraint(a, pltpu.VMEM) for a in arrays)


def mm(a, b):
    return jnp.dot(a, b, preferred_element_type=f32)


def mm_nt(a, b):
    return lax.dot_general(a, b, NT, preferred_element_type=f32)


def cost(micros):
    return pl.CostEstimate(
        flops=int(micros * 1e8), bytes_accessed=int(micros * 3e6), transcendentals=0
    )


def triangles(n):
    row = lax.broadcasted_iota(jnp.int32, (n, n), 0)
    col = lax.broadcasted_iota(jnp.int32, (n, n), 1)
    upto = jnp.where(col <= row, 1.0, 0.0).astype(bf16)
    before = jnp.where(col < row, 1.0, 0.0).astype(bf16)
    return jnp.concatenate([upto, before], axis=0)


def masks(picks, side, tri):
    values = picks.astype(jnp.int32)
    row_q = lax.broadcasted_iota(jnp.int32, (256, 128), 0)
    row_r = lax.broadcasted_iota(jnp.int32, (128, 128), 0)
    lane = lax.broadcasted_iota(jnp.int32, (128, 128), 1).astype(f32)
    place = ((((values >> 4) & 1) ^ side) << 7) + ((values >> 5) << 4) + (values & 15)
    sums = mm_nt(tri, picks)
    ends = jnp.broadcast_to(sums[:128, 8:9], (128, 128))
    starts = jnp.broadcast_to(sums[128:, 8:9], (128, 128))
    quot, rem, member = [], [], []
    for c in range(4):
        quot.append(jnp.where(row_q == place[c : c + 1], 1.0, 0.0).astype(bf16))
        rem.append(jnp.where(row_r == values[4 + c : 5 + c], 1.0, 0.0).astype(bf16))
        here = lane + float(128 * c)
        inside = (here < ends) & (here >= starts)
        member.append(jnp.where(inside, 1.0, 0.0).astype(bf16))
    return tuple(jnp.concatenate(v, axis=1) for v in (quot, rem, member))


def pool(quot, rem, member):
    composed = quot * rem
    high = composed.astype(bf16)
    low = (composed - high.astype(f32)).astype(bf16)
    return mm_nt(member, high) + mm_nt(member, low)


def pack_kernel(rows_ref, quot_ref, rem_ref, size_ref, out_ref, picks_ref, held):
    feats = rows_ref.shape[0]
    held[...] = jnp.zeros_like(held)
    for f in range(feats):
        for c in range(4):
            part = pl.ds(128 * c, 128)
            held[f, c : c + 1, :] = quot_ref[f, :, part].astype(f32)
            held[f, 4 + c : 5 + c, :] = rem_ref[f, :, part].astype(f32)
        held[f, 8:9, :] = size_ref[f].astype(f32)
    picks = held[...].astype(bf16)
    picks_ref[...] = picks
    rows = rows_ref[...]
    for z in range(out_ref.shape[0]):
        out_ref[z, :feats] = rows
        out_ref[z, feats:] = picks[2 * z : 2 * z + 2]


def pack(rows, quot, rem, sizes):
    feats, zs = rows.shape[0], rows.shape[0] // 2
    whole = lambda a: pl.BlockSpec(a.shape, lambda i: (0, 0, 0))
    pinned = in_hbm(rows, quot, rem, sizes)
    return pl.pallas_call(
        pack_kernel,
        grid=(1,),
        in_specs=[whole(a) for a in pinned],
        out_specs=[
            pl.BlockSpec((zs, feats + 2, 16, 128), lambda i: (0, 0, 0, 0)),
            pl.BlockSpec((feats, 16, 128), lambda i: (0, 0, 0)),
        ],
        out_shape=[
            jax.ShapeDtypeStruct((zs, feats + 2, 16, 128), bf16),
            jax.ShapeDtypeStruct((feats, 16, 128), bf16),
        ],
        scratch_shapes=[pltpu.VMEM((feats, 16, 128), f32)],
        compiler_params=PARAMS,
        cost_estimate=cost(1),
        name="pack",
    )(*pinned)


AHEAD = 2


def tower_kernel(mine_ref, other_ref, rem_ref, picks_ref, weight_ref, pre_ref, held, sem):
    fetch = pltpu.make_async_copy(rem_ref, held, sem)
    fetch.start()
    tri = triangles(128)
    _, side = place()
    bags, ahead, feats = [], [], rem_ref.shape[0]
    for f in range(feats + AHEAD):
        if f < feats:
            table = jnp.concatenate(
                [mine_ref[:, f].reshape(128, 128), other_ref[:, f].reshape(128, 128)], axis=0
            )
            quot_hot, rem_hot, member = masks(picks_ref[f], side, tri)
            ahead.append((mm(table.T, quot_hot), rem_hot, member))
        if f == AHEAD:
            fetch.wait()
        if f >= AHEAD:
            quot, rem_hot, member = ahead[f - AHEAD]
            bags.append(pool(quot, mm(held[f - AHEAD].T, rem_hot), member).astype(bf16))
    pre_ref[...] = mm(jnp.concatenate(bags, axis=1), weight_ref[0])


def tower_forward(mine, other, remainder, picks, weight):
    return pl.pallas_call(
        tower_kernel,
        in_specs=[vmem] * 2 + [hbm] + [vmem] * 2,
        out_specs=vmem,
        out_shape=jax.ShapeDtypeStruct((128, 256), f32),
        scratch_shapes=[pltpu.VMEM(remainder.shape, bf16), pltpu.SemaphoreType.DMA],
        compiler_params=PARAMS,
        cost_estimate=cost(6),
        name="tower_forward",
    )(mine, other, *in_hbm(remainder), picks, weight)


def place():
    shard = lax.axis_index("shard").astype(jnp.int32)
    return shard, shard & 1


def silu(pre):
    return (pre * jax.nn.sigmoid(pre)).astype(bf16).astype(f32)


def stats_kernel(pre_ref, cot_ref, gain_ref, out_ref, scaled_ref):
    act = silu(pre_ref[...])
    tower = lax.axis_index("tower").astype(jnp.int32)
    gain = gain_ref[:, pl.ds(pl.multiple_of(tower * 256, 256), 256)]
    for d in range(cot_ref.shape[0]):
        scaled_ref[4 * d : 4 * d + 4] = cot_ref[d].astype(f32) * gain
    mean = jnp.mean(act, axis=1, keepdims=True)
    center = act - mean
    scaled = scaled_ref[...]
    spread = jnp.sum(center * center, axis=1, keepdims=True)
    total = jnp.sum(scaled, axis=1, keepdims=True)
    lean = jnp.sum(scaled * center, axis=1, keepdims=True)
    lane = lax.broadcasted_iota(jnp.int32, (128, 128), 1)
    table = jnp.where(
        lane == 0, mean, jnp.where(lane == 1, spread, jnp.where(lane == 2, total, lean))
    )
    stats = table.T[:4]
    for d in range(out_ref.shape[0]):
        rows = act[4 * d : 4 * d + 4]
        out_ref[d, 0], out_ref[d, 1], out_ref[d, 2] = rows[:, :128], rows[:, 128:], stats


def local_stats(pre, cot, gain, towers):
    return pl.pallas_call(
        stats_kernel,
        in_specs=[vmem] * 3,
        out_specs=[vmem] * 2,
        out_shape=[
            jax.ShapeDtypeStruct((towers, 3, 4, 128), f32),
            jax.ShapeDtypeStruct(pre.shape, f32),
        ],
        compiler_params=PARAMS,
        cost_estimate=cost(1),
        name="local_stats",
    )(pre, cot, gain)


def norm_kernel(got_ref, gain_ref, joint_ref):
    towers = got_ref.shape[0]
    columns = float(towers * 256)
    pieces = [(t, h, pl.ds(256 * t + 128 * h, 128)) for t in range(towers) for h in range(2)]
    mean = sum(got_ref[t, h] for t, h, _ in pieces)
    mean = jnp.sum(mean, axis=1, keepdims=True) * (1.0 / columns)
    center = [got_ref[t, h] - mean for t, h, _ in pieces]
    spread = jnp.sum(sum(c * c for c in center), axis=1, keepdims=True) * (1.0 / columns)
    scale = lax.rsqrt(spread + norm_eps)
    for c, (_, _, part) in zip(center, pieces):
        joint_ref[0, :, part] = (c * scale * gain_ref[:, part]).astype(bf16)


def norm(got, gain):
    return pl.pallas_call(
        norm_kernel,
        out_shape=jax.ShapeDtypeStruct((1, 4, gain.shape[1]), bf16),
        compiler_params=PARAMS,
        cost_estimate=cost(1),
        name="norm",
    )(got, gain)


def feature_kernel(per_step, where_ref, mine_ref, other_ref, rem_ref, picks_ref, *refs):
    bag_ref, quot_ref, remd_ref, qhot_ref, rhot_ref, member_ref, qt_ref, rt_ref = refs

    @pl.when((pl.program_id(0) == 0) & (pl.program_id(1) == 0))
    def _():
        qt_ref[:, :128] = mine_ref[:, 0].reshape(128, 128).T
        qt_ref[:, 128:] = other_ref[:, 0].reshape(128, 128).T
        rt_ref[...] = rem_ref[0].T

    tri = triangles(128)
    for i in range(per_step):
        hot = masks(picks_ref[0, i], where_ref[1], tri)
        quot, rem = mm(qt_ref[...], hot[0]), mm(rt_ref[...], hot[1])
        bag_ref[0, i] = pool(quot, rem, hot[2]).T.astype(bf16)
        quot_ref[0, i], remd_ref[0, i] = quot.astype(bf16), rem.astype(bf16)
        qhot_ref[0, i], rhot_ref[0, i], member_ref[0, i] = hot


def step_block(per_step, *dims):
    return pl.BlockSpec((1, per_step, *dims), lambda h, i, w: (h, i, 0, 0))


def feature_pool(where, mine, other, remainder, picks):
    zs, per_step = picks.shape[1], 4
    table = pl.BlockSpec((zs, 1, 16, 128), lambda h, i, w: (0, w[0], 0, 0))
    sizes = [(128, 128), (128, 512), (128, 512), (256, 512), (128, 512), (128, 512)]
    return pl.pallas_call(
        functools.partial(feature_kernel, per_step),
        grid_spec=pltpu.PrefetchScalarGridSpec(
            num_scalar_prefetch=1,
            grid=(2, zs // per_step),
            in_specs=[
                table,
                table,
                pl.BlockSpec((1, 128, 128), lambda h, i, w: (w[0], 0, 0)),
                step_block(per_step, 16, 128),
            ],
            out_specs=[step_block(per_step, *s) for s in sizes],
            scratch_shapes=[pltpu.VMEM((128, 256), bf16), pltpu.VMEM((128, 128), bf16)],
        ),
        out_shape=[pltpu.HBM((2, zs, *s), bf16) for s in sizes],
        compiler_params=PARAMS,
        cost_estimate=cost(6),
        name="feature_pool",
    )(where, mine, other, *in_hbm(remainder), picks)


def back_kernel(columns, got_ref, pre_ref, scaled_ref, out_ref):
    towers = got_ref.shape[0]
    stats = got_ref[:, 2]
    sums = jnp.sum(stats, axis=0)
    mean = sums[0:1] * (1.0 / towers)
    shift = stats[:, 0:1, :] - mean[None]
    spread = sums[1:2] + (columns / towers) * jnp.sum(shift * shift, axis=0)
    lean = sums[3:4] + jnp.sum(stats[:, 2:3, :] * shift, axis=0)
    scale = lax.rsqrt(spread * (1.0 / columns) + norm_eps)
    rows = [mean, scale, sums[2:3] * (1.0 / columns), lean * scale * scale * (1.0 / columns)]
    table = jnp.concatenate(rows + [jnp.zeros((124, 128), f32)], axis=0).T
    mean, scale, total, lean = (table[:, i : i + 1] for i in range(4))
    pre = pre_ref[...]
    sigma = jax.nn.sigmoid(pre)
    grad = (scale * (scaled_ref[...] - total - (silu(pre) - mean) * lean)).astype(bf16).astype(f32)
    pre_grad = (grad * sigma * (1.0 + pre * (1.0 - sigma))).astype(bf16)
    for d in range(out_ref.shape[0]):
        out_ref[d] = pre_grad


def tower_back(got, pre, scaled, copies):
    columns = got.shape[0] * pre.shape[1]
    return pl.pallas_call(
        functools.partial(back_kernel, float(columns)),
        out_shape=jax.ShapeDtypeStruct((copies, *pre.shape), bf16),
        compiler_params=PARAMS,
        cost_estimate=cost(1),
        name="tower_back",
    )(got, pre, scaled)


CUTS = ((0, 2), (2, 4), (4, 8))


def half_sums(half, grad_ref, weight_ref, kept, held, sems, sums):
    own, _ = place()
    loads = []
    for c, (low, high) in enumerate(CUTS):
        part = pl.ds(low, high - low)
        loads.append(
            [
                pltpu.make_async_copy(a.at[half, part], b.at[part], sems.at[c, i])
                for i, (a, b) in enumerate(zip(kept, held))
            ]
        )
    for copies in loads:
        for copy in copies:
            copy.start()
    bags, quots, rems, quot_hot, rem_hot, member = held
    weight = weight_ref[0, pl.ds(pl.multiple_of(own * 128, 128), 128), :]
    weight_sum, quot_sum, rem_sum = sums
    for copies, (low, high) in zip(loads, CUTS):
        for copy in copies:
            copy.wait()
        for z in range(low, high):
            grad = grad_ref[z]
            weight_sum += mm(bags[z], grad)
            look = mm(mm_nt(weight, grad).astype(bf16), member[z])
            quot_part = (look * rems[z].astype(f32)).astype(bf16)
            rem_part = (look * quots[z].astype(f32)).astype(bf16)
            quot_sum += mm_nt(quot_part, quot_hot[z])
            rem_sum += mm_nt(rem_part, rem_hot[z])
    return weight_sum, quot_sum, rem_sum


SUMS = ((128, 256), (128, 256), (128, 128))


def first_kernel(grad_ref, weight_ref, *refs):
    kept, outs, held, sems = refs[:6], refs[6:9], refs[9:15], refs[15]
    sums = tuple(jnp.zeros(s, f32) for s in SUMS)
    for ref, value in zip(outs, half_sums(0, grad_ref, weight_ref, kept, held, sems, sums)):
        ref[...] = value


def second_kernel(grad_ref, weight_ref, *refs):
    kept, begun, out_ref, held, sems = refs[:6], refs[6:9], refs[9], refs[10:16], refs[16]
    sums = half_sums(1, grad_ref, weight_ref, kept, held, sems, tuple(ref[...] for ref in begun))
    _, side = place()
    chunk, quot, rem = sums[0].astype(bf16), sums[1].T, sums[2].T
    for z in range(out_ref.shape[0]):
        near, far = quot[16 * z : 16 * z + 16], quot[128 + 16 * z : 144 + 16 * z]
        first, second = jnp.where(side == 0, near, far), jnp.where(side == 0, far, near)
        pair = jnp.concatenate([rem[16 * z : 16 * z + 8], rem[16 * z + 8 : 16 * z + 16]], axis=1)
        rows = jnp.concatenate([jnp.concatenate([first, second], axis=1), pair], axis=0)
        out_ref[z, :128] = chunk
        out_ref[z, 128:] = rows.astype(bf16)


def grads_call(kernel, name, out_shape, grad, weight, looked, *begun):
    return pl.pallas_call(
        kernel,
        in_specs=[vmem] * 2 + [hbm] * 6 + [vmem] * len(begun),
        out_specs=jax.tree.map(lambda _: vmem, out_shape),
        out_shape=out_shape,
        scratch_shapes=[pltpu.VMEM(a.shape[1:], bf16) for a in looked]
        + [pltpu.SemaphoreType.DMA((len(CUTS), 6))],
        compiler_params=PARAMS,
        cost_estimate=cost(4),
        name=name,
    )(grad, weight, *in_hbm(*looked), *begun)


def grads_part(mine, other, weight, *looked):
    begun = [jax.ShapeDtypeStruct(s, f32) for s in SUMS]
    begun = grads_call(first_kernel, "grads_first", begun, mine, weight, looked)
    sent = jax.ShapeDtypeStruct((mine.shape[0], 152, 256), bf16)
    return grads_call(second_kernel, "grads_second", sent, other, weight, looked, *begun)


def widen_kernel(side_ref, got_ref, out_ref):
    out_ref[:, 0] = got_ref[...].astype(f32)


def widen(side, mine):
    zs, step = mine.shape[0], 4
    return pl.pallas_call(
        widen_kernel,
        grid_spec=pltpu.PrefetchScalarGridSpec(
            num_scalar_prefetch=1,
            grid=(zs // step,),
            in_specs=[pl.BlockSpec((step, 128, 256), lambda i, s: (i, 0, 0))],
            out_specs=pl.BlockSpec((step, 1, 128, 256), lambda i, s: (i, s[0], 0, 0)),
        ),
        out_shape=jax.ShapeDtypeStruct((zs, 2, 128, 256), f32),
        compiler_params=PARAMS,
        cost_estimate=cost(1),
        name="widen",
    )(side, mine)


def spread_kernel(side_ref, begun_ref, mine_ref, other_ref, weight_ref, quot_ref, rem_ref):
    side = side_ref[0]
    weight_ref[:, 0] = other_ref[:, :128].astype(f32)
    for z in range(mine_ref.shape[0]):
        for at, ref in ((side, mine_ref), (1 - side, other_ref)):
            rows = ref[z, 128:].astype(f32)
            rows = jnp.where(side == 0, rows[:, :128], rows[:, 128:])
            quot_ref[z, at] = rows[:16]
            rem_ref[z, at] = rows[16:]


def spread(side, begun, mine, other):
    zs, step = mine.shape[0], 4
    block = pl.BlockSpec((step, 152, 256), lambda i, s: (i, 0, 0))
    sizes = [(128, 256), (16, 128), (8, 128)]
    return pl.pallas_call(
        spread_kernel,
        grid_spec=pltpu.PrefetchScalarGridSpec(
            num_scalar_prefetch=1,
            grid=(zs // step,),
            in_specs=[hbm, block, block],
            out_specs=[pl.BlockSpec((step, 1, 128, 256), lambda i, s: (i, 1 - s[0], 0, 0))]
            + [pl.BlockSpec((step, 2, *s), lambda i, s: (i, 0, 0, 0)) for s in sizes[1:]],
        ),
        out_shape=[jax.ShapeDtypeStruct((zs, 2, *s), f32) for s in sizes],
        input_output_aliases={1: 0},
        compiler_params=PARAMS,
        cost_estimate=cost(2),
        name="spread",
    )(side, begun, mine, other)


def on_device(
    quotient_rows,
    remainder_rows,
    quotient_index,
    remainder_index,
    bag_sizes,
    tower_weight,
    norm_gain,
    cotangent,
):
    feats = quotient_rows.shape[0]
    shards, towers = lax.axis_size("shard"), lax.axis_size("tower")
    shard = lax.axis_index("shard")
    zs = shards // 2
    along_z = [[2 * z + c for z in range(zs)] for c in range(2)]
    across = [(i, i ^ 1) for i in range(shards)]
    swap = functools.partial(lax.all_to_all, split_axis=0, concat_axis=0, tiled=True)
    gather_z = functools.partial(swap, axis_name="shard", axis_index_groups=along_z)
    side = (shard & 1).astype(jnp.int32)
    side_arg = side[None]
    where = jnp.stack([shard, side]).astype(jnp.int32)
    packed, picks = pack(quotient_rows, quotient_index, remainder_index, bag_sizes)
    mine, late = lax.optimization_barrier((gather_z(packed), cotangent[0]))
    other = lax.ppermute(mine, "shard", across)
    late = late.reshape(4, towers, 256).transpose(1, 0, 2)
    pre = tower_forward(mine, other, remainder_rows, picks, tower_weight)
    pre, norm_gain = lax.optimization_barrier((pre, norm_gain))
    gain = norm_gain.astype(f32)[None]
    pre, gain, cot = lax.optimization_barrier((pre, gain, swap(late, "tower")))
    sent, scaled = local_stats(pre, cot, gain, towers)
    stats = swap(sent, "tower")
    grad_copies = tower_back(stats, pre, scaled, zs)
    joint = norm(stats, gain)
    all_picks = lax.dynamic_index_in_dim(
        jnp.stack([mine[:, feats:], other[:, feats:]]), side, 2, keepdims=False
    )
    looked = feature_pool(where, mine, other, remainder_rows, all_picks)
    grad_mine, joint, *looked = lax.optimization_barrier((gather_z(grad_copies), joint, *looked))
    grad_other = lax.ppermute(grad_mine, "shard", across)
    got_mine = gather_z(grads_part(grad_mine, grad_other, tower_weight, *looked))
    got_other = lax.ppermute(got_mine, "shard", across)
    begun = widen(side_arg, got_mine)
    weight_grad, quot_grad, rem_grad = spread(side_arg, begun, got_mine, got_other)
    return (
        joint,
        weight_grad.reshape(1, feats * 128, 256),
        quot_grad.reshape(feats, 16, 128),
        rem_grad.reshape(feats, 8, 128),
    )


def solution(mesh):
    in_specs = (
        P("tower", "shard", None),
        P("tower", None, None),
        P("tower", "shard", None),
        P("tower", "shard", None),
        P("tower", "shard", None),
        P("tower", None, None),
        P(),
        P("shard", "tower", None),
    )
    out_specs = (
        P("shard", "tower", None),
        P("tower", None, None),
        P("tower", "shard", None),
        P("tower", "shard", None),
    )
    return jax.shard_map(
        on_device, mesh=mesh, in_specs=in_specs, out_specs=out_specs, check_vma=False
    )
```

```python
import functools

import jax
import jax.numpy as jnp
from jax import lax
from jax.experimental import pallas as pl
from jax.experimental.pallas import tpu as pltpu
from jax.sharding import PartitionSpec as P

norm_eps = 1e-05
f32, bf16 = jnp.float32, jnp.bfloat16
NT = (((1,), (1,)), ((), ()))
PARAMS = pltpu.CompilerParams(vmem_limit_bytes=20 * 1024 * 1024)
vmem = pl.BlockSpec(memory_space=pltpu.VMEM)
hbm = pl.BlockSpec(memory_space=pltpu.HBM)


def in_hbm(*arrays):
    return tuple(pltpu.with_memory_space_constraint(a, pltpu.HBM) for a in arrays)


def mm(a, b):
    return jnp.dot(a, b, preferred_element_type=f32)


def mm_nt(a, b):
    return lax.dot_general(a, b, NT, preferred_element_type=f32)


def cost(micros):
    return pl.CostEstimate(
        flops=int(micros * 1e8), bytes_accessed=int(micros * 3e6), transcendentals=0
    )


def triangles(n):
    row = lax.broadcasted_iota(jnp.int32, (n, n), 0)
    col = lax.broadcasted_iota(jnp.int32, (n, n), 1)
    upto = jnp.where(col <= row, 1.0, 0.0).astype(bf16)
    before = jnp.where(col < row, 1.0, 0.0).astype(bf16)
    return jnp.concatenate([upto, before], axis=0)


def masks(picks, side, tri):
    values = picks.astype(jnp.int32)
    row_q = lax.broadcasted_iota(jnp.int32, (256, 128), 0)
    row_r = lax.broadcasted_iota(jnp.int32, (128, 128), 0)
    lane = lax.broadcasted_iota(jnp.int32, (128, 128), 1).astype(f32)
    place = ((((values >> 4) & 1) ^ side) << 7) + ((values >> 5) << 4) + (values & 15)
    sums = mm_nt(tri, picks)
    ends = jnp.broadcast_to(sums[:128, 8:9], (128, 128))
    starts = jnp.broadcast_to(sums[128:, 8:9], (128, 128))
    quot, rem, member = [], [], []
    for c in range(4):
        quot.append(jnp.where(row_q == place[c : c + 1], 1.0, 0.0).astype(bf16))
        rem.append(jnp.where(row_r == values[4 + c : 5 + c], 1.0, 0.0).astype(bf16))
        here = lane + float(128 * c)
        inside = (here < ends) & (here >= starts)
        member.append(jnp.where(inside, 1.0, 0.0).astype(bf16))
    return tuple(jnp.concatenate(v, axis=1) for v in (quot, rem, member))


def pool(quot, rem, member):
    composed = quot * rem
    high = composed.astype(bf16)
    low = (composed - high.astype(f32)).astype(bf16)
    return mm_nt(member, high) + mm_nt(member, low)


def pack_kernel(rows_ref, quot_ref, rem_ref, size_ref, table_ref, out_ref, picks_ref, copy_ref, held):
    copy_ref[...] = table_ref[...]
    feats = rows_ref.shape[0]
    held[...] = jnp.zeros_like(held)
    for f in range(feats):
        for c in range(4):
            part = pl.ds(128 * c, 128)
            held[f, c : c + 1, :] = quot_ref[f, :, part].astype(f32)
            held[f, 4 + c : 5 + c, :] = rem_ref[f, :, part].astype(f32)
        held[f, 8:9, :] = size_ref[f].astype(f32)
    picks = held[...].astype(bf16)
    picks_ref[...] = picks
    rows = rows_ref[...]
    for z in range(out_ref.shape[0]):
        out_ref[z, :feats] = rows
        out_ref[z, feats:] = picks[2 * z : 2 * z + 2]


def pack(rows, quot, rem, sizes, table):
    feats, zs = rows.shape[0], rows.shape[0] // 2
    whole = lambda a: pl.BlockSpec(a.shape, lambda i: (0, 0, 0))
    pinned = in_hbm(rows, quot, rem, sizes, table)
    return pl.pallas_call(
        pack_kernel,
        grid=(1,),
        in_specs=[whole(a) for a in pinned],
        out_specs=[
            pl.BlockSpec((zs, feats + 2, 16, 128), lambda i: (0, 0, 0, 0)),
            pl.BlockSpec((feats, 16, 128), lambda i: (0, 0, 0)),
            whole(table),
        ],
        out_shape=[
            jax.ShapeDtypeStruct((zs, feats + 2, 16, 128), bf16),
            jax.ShapeDtypeStruct((feats, 16, 128), bf16),
            pltpu.VMEM(table.shape, bf16),
        ],
        scratch_shapes=[pltpu.VMEM((feats, 16, 128), f32)],
        compiler_params=PARAMS,
        cost_estimate=cost(1),
        name="pack",
    )(*pinned)


def tower_kernel(mine_ref, other_ref, rem_ref, picks_ref, weight_ref, pre_ref):
    tri = triangles(128)
    _, side = place()
    bags = []
    for f in range(rem_ref.shape[0]):
        table = jnp.concatenate(
            [mine_ref[:, f].reshape(128, 128), other_ref[:, f].reshape(128, 128)], axis=0
        )
        quot_hot, rem_hot, member = masks(picks_ref[f], side, tri)
        bag = pool(mm(table.T, quot_hot), mm(rem_ref[f].T, rem_hot), member)
        bags.append(bag.astype(bf16))
    pre_ref[...] = mm(jnp.concatenate(bags, axis=1), weight_ref[0])


def tower_forward(mine, other, remainder, picks, weight):
    return pl.pallas_call(
        tower_kernel,
        in_specs=[vmem] * 5,
        out_specs=vmem,
        out_shape=jax.ShapeDtypeStruct((128, 256), f32),
        compiler_params=PARAMS,
        cost_estimate=cost(6),
        name="tower_forward",
    )(mine, other, remainder, picks, weight)


def place():
    shard = lax.axis_index("shard").astype(jnp.int32)
    return shard, shard & 1


def silu(pre):
    return (pre * jax.nn.sigmoid(pre)).astype(bf16).astype(f32)


def stats_kernel(pre_ref, cot_ref, gain_ref, out_ref, scaled_ref):
    act = silu(pre_ref[...])
    tower = lax.axis_index("tower").astype(jnp.int32)
    gain = gain_ref[:, pl.ds(pl.multiple_of(tower * 256, 256), 256)]
    for d in range(cot_ref.shape[0]):
        scaled_ref[4 * d : 4 * d + 4] = cot_ref[d].astype(f32) * gain
    mean = jnp.mean(act, axis=1, keepdims=True)
    center = act - mean
    scaled = scaled_ref[...]
    spread = jnp.sum(center * center, axis=1, keepdims=True)
    total = jnp.sum(scaled, axis=1, keepdims=True)
    lean = jnp.sum(scaled * center, axis=1, keepdims=True)
    lane = lax.broadcasted_iota(jnp.int32, (128, 128), 1)
    table = jnp.where(
        lane == 0, mean, jnp.where(lane == 1, spread, jnp.where(lane == 2, total, lean))
    )
    stats = table.T[:4]
    for d in range(out_ref.shape[0]):
        rows = act[4 * d : 4 * d + 4]
        out_ref[d, 0], out_ref[d, 1], out_ref[d, 2] = rows[:, :128], rows[:, 128:], stats


def local_stats(pre, cot, gain, towers):
    return pl.pallas_call(
        stats_kernel,
        in_specs=[vmem] * 3,
        out_specs=[vmem] * 2,
        out_shape=[
            jax.ShapeDtypeStruct((towers, 3, 4, 128), f32),
            jax.ShapeDtypeStruct(pre.shape, f32),
        ],
        compiler_params=PARAMS,
        cost_estimate=cost(1),
        name="local_stats",
    )(pre, cot, gain)


def norm_kernel(got_ref, gain_ref, joint_ref):
    towers = got_ref.shape[0]
    columns = float(towers * 256)
    pieces = [(t, h, pl.ds(256 * t + 128 * h, 128)) for t in range(towers) for h in range(2)]
    mean = sum(got_ref[t, h] for t, h, _ in pieces)
    mean = jnp.sum(mean, axis=1, keepdims=True) * (1.0 / columns)
    center = [got_ref[t, h] - mean for t, h, _ in pieces]
    spread = jnp.sum(sum(c * c for c in center), axis=1, keepdims=True) * (1.0 / columns)
    scale = lax.rsqrt(spread + norm_eps)
    for c, (_, _, part) in zip(center, pieces):
        joint_ref[0, :, part] = (c * scale * gain_ref[:, part]).astype(bf16)


def norm(got, gain):
    return pl.pallas_call(
        norm_kernel,
        out_shape=jax.ShapeDtypeStruct((1, 4, gain.shape[1]), bf16),
        compiler_params=PARAMS,
        cost_estimate=cost(1),
        name="norm",
    )(got, gain)


def feature_kernel(per_step, where_ref, mine_ref, other_ref, rem_ref, picks_ref, *refs):
    bag_ref, quot_ref, remd_ref, qhot_ref, rhot_ref, member_ref, qt_ref, rt_ref = refs

    @pl.when((pl.program_id(0) == 0) & (pl.program_id(1) == 0))
    def _():
        qt_ref[:, :128] = mine_ref[:, 0].reshape(128, 128).T
        qt_ref[:, 128:] = other_ref[:, 0].reshape(128, 128).T
        rt_ref[...] = rem_ref[0].T

    tri = triangles(128)
    for i in range(per_step):
        hot = masks(picks_ref[0, i], where_ref[1], tri)
        quot, rem = mm(qt_ref[...], hot[0]), mm(rt_ref[...], hot[1])
        bag_ref[0, i] = pool(quot, rem, hot[2]).T.astype(bf16)
        quot_ref[0, i], remd_ref[0, i] = quot.astype(bf16), rem.astype(bf16)
        qhot_ref[0, i], rhot_ref[0, i], member_ref[0, i] = hot


def step_block(per_step, *dims):
    return pl.BlockSpec((1, per_step, *dims), lambda h, i, w: (h, i, 0, 0))


def feature_pool(where, mine, other, remainder, picks):
    zs, per_step = picks.shape[1], 4
    table = pl.BlockSpec((zs, 1, 16, 128), lambda h, i, w: (0, w[0], 0, 0))
    sizes = [(128, 128), (128, 512), (128, 512), (256, 512), (128, 512), (128, 512)]
    return pl.pallas_call(
        functools.partial(feature_kernel, per_step),
        grid_spec=pltpu.PrefetchScalarGridSpec(
            num_scalar_prefetch=1,
            grid=(2, zs // per_step),
            in_specs=[
                table,
                table,
                pl.BlockSpec((1, 128, 128), lambda h, i, w: (w[0], 0, 0)),
                step_block(per_step, 16, 128),
            ],
            out_specs=[step_block(per_step, *s) for s in sizes],
            scratch_shapes=[pltpu.VMEM((128, 256), bf16), pltpu.VMEM((128, 128), bf16)],
        ),
        out_shape=[pltpu.HBM((2, zs, *s), bf16) for s in sizes],
        compiler_params=PARAMS,
        cost_estimate=cost(6),
        name="feature_pool",
    )(where, mine, other, *in_hbm(remainder), picks)


def back_kernel(columns, got_ref, pre_ref, scaled_ref, out_ref):
    towers = got_ref.shape[0]
    stats = got_ref[:, 2]
    sums = jnp.sum(stats, axis=0)
    mean = sums[0:1] * (1.0 / towers)
    shift = stats[:, 0:1, :] - mean[None]
    spread = sums[1:2] + (columns / towers) * jnp.sum(shift * shift, axis=0)
    lean = sums[3:4] + jnp.sum(stats[:, 2:3, :] * shift, axis=0)
    scale = lax.rsqrt(spread * (1.0 / columns) + norm_eps)
    rows = [mean, scale, sums[2:3] * (1.0 / columns), lean * scale * scale * (1.0 / columns)]
    table = jnp.concatenate(rows + [jnp.zeros((124, 128), f32)], axis=0).T
    mean, scale, total, lean = (table[:, i : i + 1] for i in range(4))
    pre = pre_ref[...]
    sigma = jax.nn.sigmoid(pre)
    grad = (scale * (scaled_ref[...] - total - (silu(pre) - mean) * lean)).astype(bf16).astype(f32)
    pre_grad = (grad * sigma * (1.0 + pre * (1.0 - sigma))).astype(bf16)
    for d in range(out_ref.shape[0]):
        out_ref[d] = pre_grad


def tower_back(got, pre, scaled, copies):
    columns = got.shape[0] * pre.shape[1]
    return pl.pallas_call(
        functools.partial(back_kernel, float(columns)),
        out_shape=jax.ShapeDtypeStruct((copies, *pre.shape), bf16),
        compiler_params=PARAMS,
        cost_estimate=cost(1),
        name="tower_back",
    )(got, pre, scaled)


CUTS = ((0, 2), (2, 4), (4, 8))


def half_sums(half, grad_ref, weight_ref, kept, held, sems, sums):
    own, _ = place()
    loads = []
    for c, (low, high) in enumerate(CUTS):
        part = pl.ds(low, high - low)
        loads.append(
            [
                pltpu.make_async_copy(a.at[half, part], b.at[part], sems.at[c, i])
                for i, (a, b) in enumerate(zip(kept, held))
            ]
        )
    for copies in loads:
        for copy in copies:
            copy.start()
    bags, quots, rems, quot_hot, rem_hot, member = held
    weight = weight_ref[0, pl.ds(pl.multiple_of(own * 128, 128), 128), :]
    weight_sum, quot_sum, rem_sum = sums
    for copies, (low, high) in zip(loads, CUTS):
        for copy in copies:
            copy.wait()
        for z in range(low, high):
            grad = grad_ref[z]
            weight_sum += mm(bags[z], grad)
            look = mm(mm_nt(weight, grad).astype(bf16), member[z])
            quot_part = (look * rems[z].astype(f32)).astype(bf16)
            rem_part = (look * quots[z].astype(f32)).astype(bf16)
            quot_sum += mm_nt(quot_part, quot_hot[z])
            rem_sum += mm_nt(rem_part, rem_hot[z])
    return weight_sum, quot_sum, rem_sum


SUMS = ((128, 256), (128, 256), (128, 128))


def first_kernel(grad_ref, weight_ref, *refs):
    kept, outs, held, sems = refs[:6], refs[6:9], refs[9:15], refs[15]
    sums = tuple(jnp.zeros(s, f32) for s in SUMS)
    for ref, value in zip(outs, half_sums(0, grad_ref, weight_ref, kept, held, sems, sums)):
        ref[...] = value


def second_kernel(grad_ref, weight_ref, *refs):
    kept, begun, out_ref, held, sems = refs[:6], refs[6:9], refs[9], refs[10:16], refs[16]
    sums = half_sums(1, grad_ref, weight_ref, kept, held, sems, tuple(ref[...] for ref in begun))
    _, side = place()
    chunk, quot, rem = sums[0].astype(bf16), sums[1].T, sums[2].T
    for z in range(out_ref.shape[0]):
        near, far = quot[16 * z : 16 * z + 16], quot[128 + 16 * z : 144 + 16 * z]
        first, second = jnp.where(side == 0, near, far), jnp.where(side == 0, far, near)
        pair = jnp.concatenate([rem[16 * z : 16 * z + 8], rem[16 * z + 8 : 16 * z + 16]], axis=1)
        rows = jnp.concatenate([jnp.concatenate([first, second], axis=1), pair], axis=0)
        out_ref[z, :128] = chunk
        out_ref[z, 128:] = rows.astype(bf16)


def grads_call(kernel, name, out_shape, grad, weight, looked, *begun):
    return pl.pallas_call(
        kernel,
        in_specs=[vmem] * 2 + [hbm] * 6 + [vmem] * len(begun),
        out_specs=jax.tree.map(lambda _: vmem, out_shape),
        out_shape=out_shape,
        scratch_shapes=[pltpu.VMEM(a.shape[1:], bf16) for a in looked]
        + [pltpu.SemaphoreType.DMA((len(CUTS), 6))],
        compiler_params=PARAMS,
        cost_estimate=cost(4),
        name=name,
    )(grad, weight, *in_hbm(*looked), *begun)


def grads_part(mine, other, weight, *looked):
    begun = [jax.ShapeDtypeStruct(s, f32) for s in SUMS]
    begun = grads_call(first_kernel, "grads_first", begun, mine, weight, looked)
    sent = jax.ShapeDtypeStruct((mine.shape[0], 152, 256), bf16)
    return grads_call(second_kernel, "grads_second", sent, other, weight, looked, *begun)


def widen_kernel(side_ref, got_ref, out_ref):
    out_ref[:, 0] = got_ref[...].astype(f32)


def widen(side, mine):
    zs, step = mine.shape[0], 4
    return pl.pallas_call(
        widen_kernel,
        grid_spec=pltpu.PrefetchScalarGridSpec(
            num_scalar_prefetch=1,
            grid=(zs // step,),
            in_specs=[pl.BlockSpec((step, 128, 256), lambda i, s: (i, 0, 0))],
            out_specs=pl.BlockSpec((step, 1, 128, 256), lambda i, s: (i, s[0], 0, 0)),
        ),
        out_shape=jax.ShapeDtypeStruct((zs, 2, 128, 256), f32),
        compiler_params=PARAMS,
        cost_estimate=cost(1),
        name="widen",
    )(side, mine)


def spread_kernel(side_ref, begun_ref, mine_ref, other_ref, weight_ref, quot_ref, rem_ref):
    side = side_ref[0]
    weight_ref[:, 0] = other_ref[:, :128].astype(f32)
    for z in range(mine_ref.shape[0]):
        for at, ref in ((side, mine_ref), (1 - side, other_ref)):
            rows = ref[z, 128:].astype(f32)
            rows = jnp.where(side == 0, rows[:, :128], rows[:, 128:])
            quot_ref[z, at] = rows[:16]
            rem_ref[z, at] = rows[16:]


def spread(side, begun, mine, other):
    zs, step = mine.shape[0], 4
    block = pl.BlockSpec((step, 152, 256), lambda i, s: (i, 0, 0))
    sizes = [(128, 256), (16, 128), (8, 128)]
    return pl.pallas_call(
        spread_kernel,
        grid_spec=pltpu.PrefetchScalarGridSpec(
            num_scalar_prefetch=1,
            grid=(zs // step,),
            in_specs=[hbm, block, block],
            out_specs=[pl.BlockSpec((step, 1, 128, 256), lambda i, s: (i, 1 - s[0], 0, 0))]
            + [pl.BlockSpec((step, 2, *s), lambda i, s: (i, 0, 0, 0)) for s in sizes[1:]],
        ),
        out_shape=[jax.ShapeDtypeStruct((zs, 2, *s), f32) for s in sizes],
        input_output_aliases={1: 0},
        compiler_params=PARAMS,
        cost_estimate=cost(2),
        name="spread",
    )(side, begun, mine, other)


def on_device(
    quotient_rows,
    remainder_rows,
    quotient_index,
    remainder_index,
    bag_sizes,
    tower_weight,
    norm_gain,
    cotangent,
):
    feats = quotient_rows.shape[0]
    shards, towers = lax.axis_size("shard"), lax.axis_size("tower")
    shard = lax.axis_index("shard")
    zs = shards // 2
    along_z = [[2 * z + c for z in range(zs)] for c in range(2)]
    across = [(i, i ^ 1) for i in range(shards)]
    swap = functools.partial(lax.all_to_all, split_axis=0, concat_axis=0, tiled=True)
    gather_z = functools.partial(swap, axis_name="shard", axis_index_groups=along_z)
    side = (shard & 1).astype(jnp.int32)
    side_arg = side[None]
    where = jnp.stack([shard, side]).astype(jnp.int32)
    packed, picks, tables = pack(
        quotient_rows, quotient_index, remainder_index, bag_sizes, remainder_rows
    )
    mine, late = lax.optimization_barrier((gather_z(packed), cotangent[0]))
    other = lax.ppermute(mine, "shard", across)
    late = late.reshape(4, towers, 256).transpose(1, 0, 2)
    pre = tower_forward(mine, other, tables, picks, tower_weight)
    pre, norm_gain = lax.optimization_barrier((pre, norm_gain))
    gain = norm_gain.astype(f32)[None]
    pre, gain, cot = lax.optimization_barrier((pre, gain, swap(late, "tower")))
    sent, scaled = local_stats(pre, cot, gain, towers)
    stats = swap(sent, "tower")
    grad_copies = tower_back(stats, pre, scaled, zs)
    joint = norm(stats, gain)
    all_picks = lax.dynamic_index_in_dim(
        jnp.stack([mine[:, feats:], other[:, feats:]]), side, 2, keepdims=False
    )
    looked = feature_pool(where, mine, other, remainder_rows, all_picks)
    grad_mine, joint, *looked = lax.optimization_barrier((gather_z(grad_copies), joint, *looked))
    grad_other = lax.ppermute(grad_mine, "shard", across)
    got_mine = gather_z(grads_part(grad_mine, grad_other, tower_weight, *looked))
    got_other = lax.ppermute(got_mine, "shard", across)
    begun = widen(side_arg, got_mine)
    weight_grad, quot_grad, rem_grad = spread(side_arg, begun, got_mine, got_other)
    return (
        joint,
        weight_grad.reshape(1, feats * 128, 256),
        quot_grad.reshape(feats, 16, 128),
        rem_grad.reshape(feats, 8, 128),
    )


def solution(mesh):
    in_specs = (
        P("tower", "shard", None),
        P("tower", None, None),
        P("tower", "shard", None),
        P("tower", "shard", None),
        P("tower", "shard", None),
        P("tower", None, None),
        P(),
        P("shard", "tower", None),
    )
    out_specs = (
        P("shard", "tower", None),
        P("tower", None, None),
        P("tower", "shard", None),
        P("tower", "shard", None),
    )
    return jax.shard_map(
        on_device, mesh=mesh, in_specs=in_specs, out_specs=out_specs, check_vma=False
    )
```

```python
import functools

import jax
import jax.numpy as jnp
from jax import lax
from jax.experimental import pallas as pl
from jax.experimental.pallas import tpu as pltpu
from jax.sharding import PartitionSpec as P

norm_eps = 1e-05
f32, bf16 = jnp.float32, jnp.bfloat16
NT = (((1,), (1,)), ((), ()))
PARAMS = pltpu.CompilerParams(vmem_limit_bytes=20 * 1024 * 1024)
vmem = pl.BlockSpec(memory_space=pltpu.VMEM)
hbm = pl.BlockSpec(memory_space=pltpu.HBM)


def in_hbm(*arrays):
    return tuple(pltpu.with_memory_space_constraint(a, pltpu.HBM) for a in arrays)


def mm(a, b):
    return jnp.dot(a, b, preferred_element_type=f32)


def mm_nt(a, b):
    return lax.dot_general(a, b, NT, preferred_element_type=f32)


def cost(micros):
    return pl.CostEstimate(
        flops=int(micros * 1e8), bytes_accessed=int(micros * 3e6), transcendentals=0
    )


def triangles(n):
    row = lax.broadcasted_iota(jnp.int32, (n, n), 0)
    col = lax.broadcasted_iota(jnp.int32, (n, n), 1)
    upto = jnp.where(col <= row, 1.0, 0.0).astype(bf16)
    before = jnp.where(col < row, 1.0, 0.0).astype(bf16)
    return jnp.concatenate([upto, before], axis=0)


def one_hots(picks, side):
    values = picks.astype(jnp.int32)
    row_q = lax.broadcasted_iota(jnp.int32, (256, 128), 0)
    row_r = lax.broadcasted_iota(jnp.int32, (128, 128), 0)
    spot = ((((values >> 4) & 1) ^ side) << 7) + ((values >> 5) << 4) + (values & 15)
    quot, rem = [], []
    for c in range(4):
        quot.append(jnp.where(row_q == spot[c : c + 1], 1.0, 0.0).astype(bf16))
        rem.append(jnp.where(row_r == values[4 + c : 5 + c], 1.0, 0.0).astype(bf16))
    return jnp.concatenate(quot, axis=1), jnp.concatenate(rem, axis=1)


def masks(picks, side, tri):
    lane = lax.broadcasted_iota(jnp.int32, (128, 128), 1).astype(f32)
    sums = mm_nt(tri, picks)
    ends = jnp.broadcast_to(sums[:128, 8:9], (128, 128))
    starts = jnp.broadcast_to(sums[128:, 8:9], (128, 128))
    member = []
    for c in range(4):
        here = lane + float(128 * c)
        inside = (here < ends) & (here >= starts)
        member.append(jnp.where(inside, 1.0, 0.0).astype(bf16))
    return *one_hots(picks, side), jnp.concatenate(member, axis=1)


def pool(quot, rem, member):
    composed = quot * rem
    high = composed.astype(bf16)
    low = (composed - high.astype(f32)).astype(bf16)
    return mm_nt(member, high) + mm_nt(member, low)


def pack_kernel(rows_ref, quot_ref, rem_ref, size_ref, table_ref, out_ref, picks_ref, copy_ref, held):
    copy_ref[...] = table_ref[...]
    feats = rows_ref.shape[0]
    held[...] = jnp.zeros_like(held)
    for f in range(feats):
        for c in range(4):
            part = pl.ds(128 * c, 128)
            held[f, c : c + 1, :] = quot_ref[f, :, part].astype(f32)
            held[f, 4 + c : 5 + c, :] = rem_ref[f, :, part].astype(f32)
        held[f, 8:9, :] = size_ref[f].astype(f32)
    picks = held[...].astype(bf16)
    picks_ref[...] = picks
    rows = rows_ref[...]
    for z in range(out_ref.shape[0]):
        out_ref[z, :feats] = rows
        out_ref[z, feats:] = picks[2 * z : 2 * z + 2]


def pack(rows, quot, rem, sizes, table):
    feats, zs = rows.shape[0], rows.shape[0] // 2
    whole = lambda a: pl.BlockSpec(a.shape, lambda i: (0, 0, 0))
    pinned = in_hbm(rows, quot, rem, sizes, table)
    return pl.pallas_call(
        pack_kernel,
        grid=(1,),
        in_specs=[whole(a) for a in pinned],
        out_specs=[
            pl.BlockSpec((zs, feats + 2, 16, 128), lambda i: (0, 0, 0, 0)),
            pl.BlockSpec((feats, 16, 128), lambda i: (0, 0, 0)),
            whole(table),
        ],
        out_shape=[
            jax.ShapeDtypeStruct((zs, feats + 2, 16, 128), bf16),
            jax.ShapeDtypeStruct((feats, 16, 128), bf16),
            pltpu.VMEM(table.shape, bf16),
        ],
        scratch_shapes=[pltpu.VMEM((feats, 16, 128), f32)],
        compiler_params=PARAMS,
        cost_estimate=cost(1),
        name="pack",
    )(*pinned)


def tower_kernel(mine_ref, other_ref, rem_ref, picks_ref, weight_ref, pre_ref):
    tri = triangles(128)
    _, side = place()
    bags = []
    for f in range(rem_ref.shape[0]):
        table = jnp.concatenate(
            [mine_ref[:, f].reshape(128, 128), other_ref[:, f].reshape(128, 128)], axis=0
        )
        quot_hot, rem_hot, member = masks(picks_ref[f], side, tri)
        bag = pool(mm(table.T, quot_hot), mm(rem_ref[f].T, rem_hot), member)
        bags.append(bag.astype(bf16))
    pre_ref[...] = mm(jnp.concatenate(bags, axis=1), weight_ref[0])


def tower_forward(mine, other, remainder, picks, weight):
    return pl.pallas_call(
        tower_kernel,
        in_specs=[vmem] * 5,
        out_specs=vmem,
        out_shape=jax.ShapeDtypeStruct((128, 256), f32),
        compiler_params=PARAMS,
        cost_estimate=cost(6),
        name="tower_forward",
    )(mine, other, remainder, picks, weight)


def place():
    shard = lax.axis_index("shard").astype(jnp.int32)
    return shard, shard & 1


def silu(pre):
    return (pre * jax.nn.sigmoid(pre)).astype(bf16).astype(f32)


def stats_kernel(pre_ref, cot_ref, gain_ref, out_ref, scaled_ref):
    act = silu(pre_ref[...])
    tower = lax.axis_index("tower").astype(jnp.int32)
    gain = gain_ref[:, pl.ds(pl.multiple_of(tower * 256, 256), 256)]
    for d in range(cot_ref.shape[0]):
        scaled_ref[4 * d : 4 * d + 4] = cot_ref[d].astype(f32) * gain
    mean = jnp.mean(act, axis=1, keepdims=True)
    center = act - mean
    scaled = scaled_ref[...]
    spread = jnp.sum(center * center, axis=1, keepdims=True)
    total = jnp.sum(scaled, axis=1, keepdims=True)
    lean = jnp.sum(scaled * center, axis=1, keepdims=True)
    lane = lax.broadcasted_iota(jnp.int32, (128, 128), 1)
    table = jnp.where(
        lane == 0, mean, jnp.where(lane == 1, spread, jnp.where(lane == 2, total, lean))
    )
    stats = table.T[:4]
    for d in range(out_ref.shape[0]):
        rows = act[4 * d : 4 * d + 4]
        out_ref[d, 0], out_ref[d, 1], out_ref[d, 2] = rows[:, :128], rows[:, 128:], stats


def local_stats(pre, cot, gain, towers):
    return pl.pallas_call(
        stats_kernel,
        in_specs=[vmem] * 3,
        out_specs=[vmem] * 2,
        out_shape=[
            jax.ShapeDtypeStruct((towers, 3, 4, 128), f32),
            jax.ShapeDtypeStruct(pre.shape, f32),
        ],
        compiler_params=PARAMS,
        cost_estimate=cost(1),
        name="local_stats",
    )(pre, cot, gain)


def norm_kernel(got_ref, gain_ref, joint_ref):
    towers = got_ref.shape[0]
    columns = float(towers * 256)
    pieces = [(t, h, pl.ds(256 * t + 128 * h, 128)) for t in range(towers) for h in range(2)]
    mean = sum(got_ref[t, h] for t, h, _ in pieces)
    mean = jnp.sum(mean, axis=1, keepdims=True) * (1.0 / columns)
    center = [got_ref[t, h] - mean for t, h, _ in pieces]
    spread = jnp.sum(sum(c * c for c in center), axis=1, keepdims=True) * (1.0 / columns)
    scale = lax.rsqrt(spread + norm_eps)
    for c, (_, _, part) in zip(center, pieces):
        joint_ref[0, :, part] = (c * scale * gain_ref[:, part]).astype(bf16)


def norm(got, gain):
    return pl.pallas_call(
        norm_kernel,
        out_shape=jax.ShapeDtypeStruct((1, 4, gain.shape[1]), bf16),
        compiler_params=PARAMS,
        cost_estimate=cost(1),
        name="norm",
    )(got, gain)


def feature_kernel(per_step, where_ref, mine_ref, other_ref, rem_ref, picks_ref, *refs):
    bag_ref, quot_ref, remd_ref, member_ref, qt_ref, rt_ref = refs

    @pl.when((pl.program_id(0) == 0) & (pl.program_id(1) == 0))
    def _():
        qt_ref[:, :128] = mine_ref[:, 0].reshape(128, 128).T
        qt_ref[:, 128:] = other_ref[:, 0].reshape(128, 128).T
        rt_ref[...] = rem_ref[0].T

    tri = triangles(128)
    for i in range(per_step):
        hot = masks(picks_ref[0, i], where_ref[1], tri)
        quot, rem = mm(qt_ref[...], hot[0]), mm(rt_ref[...], hot[1])
        bag_ref[0, i] = pool(quot, rem, hot[2]).T.astype(bf16)
        quot_ref[0, i], remd_ref[0, i] = quot.astype(bf16), rem.astype(bf16)
        member_ref[0, i] = hot[2]


def step_block(per_step, *dims):
    return pl.BlockSpec((1, per_step, *dims), lambda h, i, w: (h, i, 0, 0))


def feature_pool(where, mine, other, remainder, picks):
    zs, per_step = picks.shape[1], 4
    table = pl.BlockSpec((zs, 1, 16, 128), lambda h, i, w: (0, w[0], 0, 0))
    sizes = [(128, 128), (128, 512), (128, 512), (128, 512)]
    return pl.pallas_call(
        functools.partial(feature_kernel, per_step),
        grid_spec=pltpu.PrefetchScalarGridSpec(
            num_scalar_prefetch=1,
            grid=(2, zs // per_step),
            in_specs=[
                table,
                table,
                pl.BlockSpec((1, 128, 128), lambda h, i, w: (w[0], 0, 0)),
                step_block(per_step, 16, 128),
            ],
            out_specs=[step_block(per_step, *s) for s in sizes],
            scratch_shapes=[pltpu.VMEM((128, 256), bf16), pltpu.VMEM((128, 128), bf16)],
        ),
        out_shape=[pltpu.HBM((2, zs, *s), bf16) for s in sizes],
        compiler_params=PARAMS,
        cost_estimate=cost(6),
        name="feature_pool",
    )(where, mine, other, *in_hbm(remainder), picks)


def back_kernel(columns, got_ref, pre_ref, scaled_ref, out_ref):
    towers = got_ref.shape[0]
    stats = got_ref[:, 2]
    sums = jnp.sum(stats, axis=0)
    mean = sums[0:1] * (1.0 / towers)
    shift = stats[:, 0:1, :] - mean[None]
    spread = sums[1:2] + (columns / towers) * jnp.sum(shift * shift, axis=0)
    lean = sums[3:4] + jnp.sum(stats[:, 2:3, :] * shift, axis=0)
    scale = lax.rsqrt(spread * (1.0 / columns) + norm_eps)
    rows = [mean, scale, sums[2:3] * (1.0 / columns), lean * scale * scale * (1.0 / columns)]
    table = jnp.concatenate(rows + [jnp.zeros((124, 128), f32)], axis=0).T
    mean, scale, total, lean = (table[:, i : i + 1] for i in range(4))
    pre = pre_ref[...]
    sigma = jax.nn.sigmoid(pre)
    grad = (scale * (scaled_ref[...] - total - (silu(pre) - mean) * lean)).astype(bf16).astype(f32)
    pre_grad = (grad * sigma * (1.0 + pre * (1.0 - sigma))).astype(bf16)
    for d in range(out_ref.shape[0]):
        out_ref[d] = pre_grad


def tower_back(got, pre, scaled, copies):
    columns = got.shape[0] * pre.shape[1]
    return pl.pallas_call(
        functools.partial(back_kernel, float(columns)),
        out_shape=jax.ShapeDtypeStruct((copies, *pre.shape), bf16),
        compiler_params=PARAMS,
        cost_estimate=cost(1),
        name="tower_back",
    )(got, pre, scaled)


CUTS = ((0, 2), (2, 4), (4, 8))


def half_sums(half, grad_ref, got_ref, weight_ref, kept, held, sems, sums):
    own, side = place()
    feats = 2 * got_ref.shape[0]
    loads = []
    for c, (low, high) in enumerate(CUTS):
        part = pl.ds(low, high - low)
        loads.append(
            [
                pltpu.make_async_copy(a.at[half, part], b.at[part], sems.at[c, i])
                for i, (a, b) in enumerate(zip(kept, held))
            ]
        )
    for copies in loads:
        for copy in copies:
            copy.start()
    bags, quots, rems, member = held
    weight = weight_ref[0, pl.ds(pl.multiple_of(own * 128, 128), 128), :]
    weight_sum, quot_sum, rem_sum = sums
    for copies, (low, high) in zip(loads, CUTS):
        for copy in copies:
            copy.wait()
        for z in range(low, high):
            grad = grad_ref[z]
            weight_sum += mm(bags[z], grad)
            look = mm(mm_nt(weight, grad).astype(bf16), member[z])
            quot_part = (look * rems[z].astype(f32)).astype(bf16)
            rem_part = (look * quots[z].astype(f32)).astype(bf16)
            quot_hot, rem_hot = one_hots(got_ref[z, feats + side], side)
            quot_sum += mm_nt(quot_part, quot_hot)
            rem_sum += mm_nt(rem_part, rem_hot)
    return weight_sum, quot_sum, rem_sum


SUMS = ((128, 256), (128, 256), (128, 128))


def first_kernel(grad_ref, got_ref, weight_ref, *refs):
    kept, outs, held, sems = refs[:4], refs[4:7], refs[7:11], refs[11]
    sums = tuple(jnp.zeros(s, f32) for s in SUMS)
    for ref, value in zip(outs, half_sums(0, grad_ref, got_ref, weight_ref, kept, held, sems, sums)):
        ref[...] = value


def second_kernel(grad_ref, got_ref, weight_ref, *refs):
    kept, begun, out_ref, held, sems = refs[:4], refs[4:7], refs[7], refs[8:12], refs[12]
    sums = tuple(ref[...] for ref in begun)
    sums = half_sums(1, grad_ref, got_ref, weight_ref, kept, held, sems, sums)
    _, side = place()
    chunk, quot, rem = sums[0].astype(bf16), sums[1].T, sums[2].T
    for z in range(out_ref.shape[0]):
        near, far = quot[16 * z : 16 * z + 16], quot[128 + 16 * z : 144 + 16 * z]
        first, second = jnp.where(side == 0, near, far), jnp.where(side == 0, far, near)
        pair = jnp.concatenate([rem[16 * z : 16 * z + 8], rem[16 * z + 8 : 16 * z + 16]], axis=1)
        rows = jnp.concatenate([jnp.concatenate([first, second], axis=1), pair], axis=0)
        out_ref[z, :128] = chunk
        out_ref[z, 128:] = rows.astype(bf16)


def grads_call(kernel, name, out_shape, grad, got, weight, looked, *begun):
    return pl.pallas_call(
        kernel,
        in_specs=[vmem] * 3 + [hbm] * 4 + [vmem] * len(begun),
        out_specs=jax.tree.map(lambda _: vmem, out_shape),
        out_shape=out_shape,
        scratch_shapes=[pltpu.VMEM(a.shape[1:], bf16) for a in looked]
        + [pltpu.SemaphoreType.DMA((len(CUTS), 4))],
        compiler_params=PARAMS,
        cost_estimate=cost(4),
        name=name,
    )(grad, got, weight, *in_hbm(*looked), *begun)


def grads_part(mine, other, got_mine, got_other, weight, *looked):
    begun = [jax.ShapeDtypeStruct(s, f32) for s in SUMS]
    begun = grads_call(first_kernel, "grads_first", begun, mine, got_mine, weight, looked)
    sent = jax.ShapeDtypeStruct((mine.shape[0], 152, 256), bf16)
    return grads_call(second_kernel, "grads_second", sent, other, got_other, weight, looked, *begun)


def widen_kernel(side_ref, got_ref, out_ref):
    out_ref[:, 0] = got_ref[...].astype(f32)


def widen(side, mine):
    zs, step = mine.shape[0], 4
    return pl.pallas_call(
        widen_kernel,
        grid_spec=pltpu.PrefetchScalarGridSpec(
            num_scalar_prefetch=1,
            grid=(zs // step,),
            in_specs=[pl.BlockSpec((step, 128, 256), lambda i, s: (i, 0, 0))],
            out_specs=pl.BlockSpec((step, 1, 128, 256), lambda i, s: (i, s[0], 0, 0)),
        ),
        out_shape=jax.ShapeDtypeStruct((zs, 2, 128, 256), f32),
        compiler_params=PARAMS,
        cost_estimate=cost(1),
        name="widen",
    )(side, mine)


def spread_kernel(side_ref, begun_ref, mine_ref, other_ref, weight_ref, quot_ref, rem_ref):
    side = side_ref[0]
    weight_ref[:, 0] = other_ref[:, :128].astype(f32)
    for z in range(mine_ref.shape[0]):
        for at, ref in ((side, mine_ref), (1 - side, other_ref)):
            rows = ref[z, 128:].astype(f32)
            rows = jnp.where(side == 0, rows[:, :128], rows[:, 128:])
            quot_ref[z, at] = rows[:16]
            rem_ref[z, at] = rows[16:]


def spread(side, begun, mine, other):
    zs, step = mine.shape[0], 4
    block = pl.BlockSpec((step, 152, 256), lambda i, s: (i, 0, 0))
    sizes = [(128, 256), (16, 128), (8, 128)]
    return pl.pallas_call(
        spread_kernel,
        grid_spec=pltpu.PrefetchScalarGridSpec(
            num_scalar_prefetch=1,
            grid=(zs // step,),
            in_specs=[hbm, block, block],
            out_specs=[pl.BlockSpec((step, 1, 128, 256), lambda i, s: (i, 1 - s[0], 0, 0))]
            + [pl.BlockSpec((step, 2, *s), lambda i, s: (i, 0, 0, 0)) for s in sizes[1:]],
        ),
        out_shape=[jax.ShapeDtypeStruct((zs, 2, *s), f32) for s in sizes],
        input_output_aliases={1: 0},
        compiler_params=PARAMS,
        cost_estimate=cost(2),
        name="spread",
    )(side, begun, mine, other)


def on_device(
    quotient_rows,
    remainder_rows,
    quotient_index,
    remainder_index,
    bag_sizes,
    tower_weight,
    norm_gain,
    cotangent,
):
    feats = quotient_rows.shape[0]
    shards, towers = lax.axis_size("shard"), lax.axis_size("tower")
    shard = lax.axis_index("shard")
    zs = shards // 2
    along_z = [[2 * z + c for z in range(zs)] for c in range(2)]
    across = [(i, i ^ 1) for i in range(shards)]
    swap = functools.partial(lax.all_to_all, split_axis=0, concat_axis=0, tiled=True)
    gather_z = functools.partial(swap, axis_name="shard", axis_index_groups=along_z)
    side = (shard & 1).astype(jnp.int32)
    side_arg = side[None]
    where = jnp.stack([shard, side]).astype(jnp.int32)
    packed, picks, tables = pack(
        quotient_rows, quotient_index, remainder_index, bag_sizes, remainder_rows
    )
    mine, late = lax.optimization_barrier((gather_z(packed), cotangent[0]))
    other = lax.ppermute(mine, "shard", across)
    late = late.reshape(4, towers, 256).transpose(1, 0, 2)
    pre = tower_forward(mine, other, tables, picks, tower_weight)
    pre, norm_gain = lax.optimization_barrier((pre, norm_gain))
    gain = norm_gain.astype(f32)[None]
    pre, gain, cot = lax.optimization_barrier((pre, gain, swap(late, "tower")))
    sent, scaled = local_stats(pre, cot, gain, towers)
    stats = swap(sent, "tower")
    grad_copies = tower_back(stats, pre, scaled, zs)
    joint = norm(stats, gain)
    all_picks = lax.dynamic_index_in_dim(
        jnp.stack([mine[:, feats:], other[:, feats:]]), side, 2, keepdims=False
    )
    looked = feature_pool(where, mine, other, remainder_rows, all_picks)
    grad_mine, joint, *looked = lax.optimization_barrier((gather_z(grad_copies), joint, *looked))
    grad_other = lax.ppermute(grad_mine, "shard", across)
    got_mine = gather_z(grads_part(grad_mine, grad_other, mine, other, tower_weight, *looked))
    got_other = lax.ppermute(got_mine, "shard", across)
    begun = widen(side_arg, got_mine)
    weight_grad, quot_grad, rem_grad = spread(side_arg, begun, got_mine, got_other)
    return (
        joint,
        weight_grad.reshape(1, feats * 128, 256),
        quot_grad.reshape(feats, 16, 128),
        rem_grad.reshape(feats, 8, 128),
    )


def solution(mesh):
    in_specs = (
        P("tower", "shard", None),
        P("tower", None, None),
        P("tower", "shard", None),
        P("tower", "shard", None),
        P("tower", "shard", None),
        P("tower", None, None),
        P(),
        P("shard", "tower", None),
    )
    out_specs = (
        P("shard", "tower", None),
        P("tower", None, None),
        P("tower", "shard", None),
        P("tower", "shard", None),
    )
    return jax.shard_map(
        on_device, mesh=mesh, in_specs=in_specs, out_specs=out_specs, check_vma=False
    )
```
